32 devices in a mesh: grp: 2 (over x), rows: 8 (over z, y), cols: 2 (over core).
Axes of the slice: x: 2, y: 2, z: 4, core: 2. Of those that a mesh axis runs over, the one named last changes fastest.
Arguments:
- crop_feature_grid: bfloat16 [128, 256, 512], P(('grp', 'rows'), 'cols'), parts along dimension 0, may hold values from -6 to 6
- pixel_layernorm_gain: float32 [512], replicated, may hold values from 0.25 to 1.75
- triple_projection_matrix: bfloat16 [512, 1536], replicated, may hold values from -0.25 to 0.25
- halo_exit_matrix: bfloat16 [512, 512], replicated, may hold values from -0.25 to 0.25
- memory_slots: bfloat16 [256, 512], replicated, may hold values from -6 to 6
- memory_layernorm_gain: float32 [512], replicated, may hold values from 0.25 to 1.75
- memory_asking_matrix: bfloat16 [512, 512], replicated, may hold values from -0.25 to 0.25
- memory_exit_matrix: bfloat16 [512, 512], replicated, may hold values from -0.25 to 0.25
- branch_logit_multiplier: float32 [8], replicated, may hold values from 1 to 30, as said below
Outputs:
- tokens_out: bfloat16 [128, 256, 512], P(('grp', 'rows'), 'cols'), parts along dimension 0
- latent_mix: bfloat16 [512, 512], P('grp'), parts along dimension 0
The draws below stay inside these ranges and needn't reach their ends.
There are 2 independent parts, one for each index of `grp`. The reference program is written for one: setup_inputs(seed, part) draws one part's arguments, and reference() takes and returns one part's arrays. A program takes and returns all parts, laid end to end along the dimension named above; an argument that names none is the same for every part. Nothing has to cross between parts.
Inputs may be any that keep to these rules, and one draw needn't show every extreme that they name: `branch_logit_multiplier`: a positive logit scale for each head.
All inputs are finite; a program needn't handle non-finite values.
Results may differ from the reference program's by a relative error of at most 0.0095.
The reference program's roundings to bfloat16 on the way (of `normed`, `weights`, `attended`, `latent_queries` and `latent_attended`) count: a program that leaves them out, or rounds other values in their place, can miss the bound.
Values may be sent and summed in bfloat16 or wider, within the bound.
No kernel may reach another device: no remote copies, remote signals or barrier semaphores. Data moves between devices by JAX's collectives and lax.ppermute only.
A program may use at most 192 MiB of HBM per device.

```python
import math
import jax
import jax.numpy as jnp
from jax import lax

H = 8
D = 512
L = 256
BLK = 8
RIM = 3
HH = 64
WW = 256


def draw_branch_logit_multiplier(key, part):
    lower_end = 0.0
    upper_end = math.log(6.0)
    return jnp.exp(jax.random.uniform(key, (H,), jnp.float32, lower_end, upper_end))


def steps_of(own_key, dims, shards, smallest, high):
    level, own = 1.0, jax.random.fold_in(own_key, 6)
    for axis_at, parts in shards:
        steps = jnp.exp(jax.random.uniform(jax.random.fold_in(own, axis_at), (parts,), jnp.float32, smallest / len(shards), high / len(shards)))
        level = level * jnp.repeat(steps, dims[axis_at] // parts).reshape([-1 if axis == axis_at else 1 for axis in range(len(dims))])
    return level


def scatter_about(stream_key, extent, deviation, reach, pieces=(), kind=jnp.bfloat16):
    drawn = jax.random.normal(stream_key, extent, jnp.float32) * deviation
    if len(pieces) > 0:
        drawn = steps_of(stream_key, extent, pieces, -0.22, 0.18) * drawn
    return jnp.clip(drawn, min=-reach, max=reach).astype(kind)


def setup_inputs(seed: int = 0, part: int = 0) -> dict:
    streams_of = jax.random.split(jax.random.key(seed), 10)
    part_splits = jax.random.split(jax.random.fold_in(streams_of[9], part), 10)
    return {
        "crop_feature_grid": scatter_about(part_splits[0], (HH, WW, D), 1.0, 6.0, ((0, 8), (1, 2))),
        "pixel_layernorm_gain": jnp.clip(1.0 + 0.15 * jax.random.normal(streams_of[1], (D,), jnp.float32), 0.25, 1.75),
        "triple_projection_matrix": scatter_about(streams_of[2], (D, 3 * D), D ** -0.5, 0.25),
        "halo_exit_matrix": scatter_about(streams_of[3], (D, D), D ** -0.5, 0.25),
        "memory_slots": scatter_about(streams_of[4], (L, D), 1.0, 6.0),
        "memory_layernorm_gain": jnp.clip(1.0 + 0.15 * jax.random.normal(streams_of[5], (D,), jnp.float32), 0.25, 1.75),
        "memory_asking_matrix": scatter_about(streams_of[6], (D, D), D ** -0.5, 0.25),
        "memory_exit_matrix": scatter_about(streams_of[7], (D, D), D ** -0.5, 0.25),
        "branch_logit_multiplier": draw_branch_logit_multiplier(jax.random.fold_in(streams_of[9], 71), part),
    }


def row_norm(values, gain_vector):
    floats = values.astype(jnp.float32)
    scaled = floats * lax.rsqrt(lax.optimization_barrier(jnp.mean(floats * floats, axis=-1, keepdims=True)) + 1e-05)
    return (scaled * gain_vector.astype(jnp.float32)).astype(jnp.bfloat16)

def head_norm(floats, head_count):
    shaped = floats.reshape(floats.shape[:-1] + (head_count, floats.shape[-1] // head_count))
    normal = shaped * lax.rsqrt(lax.optimization_barrier(jnp.mean(shaped * shaped, axis=-1, keepdims=True)) + 1e-06)
    return normal.astype(jnp.bfloat16)

def halo_attention(queries, keys_ext, values_ext, inside, logit_divisor):
    rows_all, cols_all, head_count, channels_per_branch = queries.shape
    blocks_across = cols_all // BLK
    window = BLK + 2 * RIM
    offsets = (jnp.arange(blocks_across, dtype=jnp.int32) * BLK)[:, None] + jnp.arange(window, dtype=jnp.int32)[None, :]

    def one_row(block_row):
        first_row = (block_row * BLK).astype(jnp.int32)
        query_rows = lax.dynamic_slice_in_dim(queries, first_row, BLK, 0)
        query_blocks = query_rows.reshape(BLK, blocks_across, BLK, head_count, channels_per_branch)
        query_blocks = query_blocks.transpose(1, 0, 2, 3, 4).reshape(blocks_across, BLK * BLK, head_count, channels_per_branch)
        key_slab = lax.dynamic_slice_in_dim(keys_ext, first_row, window, 0)[:, offsets]
        key_blocks = key_slab.transpose(1, 0, 2, 3, 4).reshape(blocks_across, window * window, head_count, channels_per_branch)
        value_slab = lax.dynamic_slice_in_dim(values_ext, first_row, window, 0)[:, offsets]
        value_blocks = value_slab.transpose(1, 0, 2, 3, 4).reshape(blocks_across, window * window, head_count, channels_per_branch)
        mask_slab = lax.dynamic_slice_in_dim(inside, first_row, window, 0)[:, offsets]
        mask_blocks = mask_slab.transpose(1, 0, 2).reshape(blocks_across, window * window)
        scores = jnp.einsum('bqhd,bkhd->bhqk', query_blocks.astype(jnp.float32), key_blocks.astype(jnp.float32))
        scores = scores * logit_divisor[None, :, None, None]
        scores = jnp.where(mask_blocks[:, None, None, :], scores, -1e+30)
        row_peak = lax.optimization_barrier(jnp.max(scores, axis=-1, keepdims=True))
        expo = jnp.exp(scores - row_peak)
        row_total = lax.optimization_barrier(jnp.sum(expo, axis=-1))
        weights = expo.astype(jnp.bfloat16)
        output = jnp.einsum('bhqk,bkhd->bqhd', weights.astype(jnp.float32), value_blocks.astype(jnp.float32))
        output = output / row_total.transpose(0, 2, 1)[..., None]
        output = output.reshape(blocks_across, BLK, BLK, head_count * channels_per_branch).transpose(1, 0, 2, 3)
        return output.reshape(BLK, cols_all, head_count * channels_per_branch).astype(jnp.bfloat16)
    result = lax.map(one_row, jnp.arange(rows_all // BLK, dtype=jnp.int32))
    return result.reshape(rows_all, cols_all, head_count * channels_per_branch)

def reference(crop_feature_grid, pixel_layernorm_gain, triple_projection_matrix, halo_exit_matrix, memory_slots, memory_layernorm_gain, memory_asking_matrix, memory_exit_matrix, branch_logit_multiplier):
    rows_all, cols_all, model_width = crop_feature_grid.shape
    channels_per_branch = model_width // H
    normed = row_norm(crop_feature_grid, pixel_layernorm_gain)
    projected = jnp.dot(normed.reshape(-1, model_width), triple_projection_matrix, preferred_element_type=jnp.float32)
    projected = projected.reshape(rows_all, cols_all, 3 * model_width)
    queries = head_norm(projected[..., :model_width], H)
    keys = head_norm(projected[..., model_width:2 * model_width], H)
    values = projected[..., 2 * model_width:].reshape(rows_all, cols_all, H, channels_per_branch).astype(jnp.bfloat16)
    logit_divisor = branch_logit_multiplier.astype(jnp.float32) / math.sqrt(channels_per_branch)
    padding = ((RIM, RIM), (RIM, RIM), (0, 0), (0, 0))
    keys_ext = jnp.pad(keys, padding)
    values_ext = jnp.pad(values, padding)
    inside = jnp.pad(jnp.ones((rows_all, cols_all), dtype=bool), ((RIM, RIM), (RIM, RIM)))
    attended = halo_attention(queries, keys_ext, values_ext, inside, logit_divisor)
    branch = jnp.dot(attended.reshape(-1, model_width), halo_exit_matrix, preferred_element_type=jnp.float32)
    tokens_out = (crop_feature_grid.astype(jnp.float32) + branch.reshape(rows_all, cols_all, model_width)).astype(jnp.bfloat16)
    latent_normed = row_norm(memory_slots, memory_layernorm_gain)
    latent_queries = head_norm(jnp.dot(latent_normed, memory_asking_matrix, preferred_element_type=jnp.float32), H)
    keys_heads = keys.reshape(-1, H, channels_per_branch).transpose(1, 0, 2)
    values_heads = values.reshape(-1, H, channels_per_branch).transpose(1, 0, 2)

    def one_head(operands):
        query_head, key_head, value_head, head_scale = operands
        scores = jnp.dot(query_head, key_head.T, preferred_element_type=jnp.float32) * head_scale
        row_peak = lax.optimization_barrier(jnp.max(scores, axis=-1, keepdims=True))
        expo = jnp.exp(scores - row_peak)
        row_total = lax.optimization_barrier(jnp.sum(expo, axis=-1, keepdims=True))
        weighted = jnp.dot(expo.astype(jnp.bfloat16), value_head, preferred_element_type=jnp.float32)
        return weighted / row_total
    latent_heads = lax.map(one_head, (latent_queries.transpose(1, 0, 2), keys_heads, values_heads, logit_divisor))
    latent_attended = latent_heads.transpose(1, 0, 2).reshape(L, model_width).astype(jnp.bfloat16)
    latent_mix = jnp.dot(latent_attended, memory_exit_matrix, preferred_element_type=jnp.float32).astype(jnp.bfloat16)
    return (tokens_out, latent_mix)
```

```python
import math

import jax
import jax.numpy as jnp
from jax import lax
from jax.experimental import pallas as pl
from jax.experimental.pallas import tpu as pltpu
from jax.sharding import PartitionSpec as P

H = 8
BLK = 8
RIM = 3
LOG2E = math.log2(math.e)
F32 = jnp.float32
BF16 = jnp.bfloat16
NEG = -1e30
VMEM = pl.BlockSpec(memory_space=pltpu.VMEM)
SMEM = pl.BlockSpec(memory_space=pltpu.SMEM)
CONTRACT_LAST = (((1,), (1,)), ((), ()))


def dot(a, b):
    return jnp.dot(a, b, preferred_element_type=F32)


def token_norm(floats, gain):
    scaled = floats * lax.rsqrt(jnp.mean(floats * floats, axis=-1, keepdims=True) + 1e-05)
    return (scaled * gain).astype(BF16)


def head_ones(width, channels):
    a = lax.broadcasted_iota(jnp.int32, (width, width), 0) // channels
    b = lax.broadcasted_iota(jnp.int32, (width, width), 1) // channels
    return jnp.where(a == b, 1.0, 0.0).astype(BF16)


def head_norm(floats, ones, channels):
    squares = floats * floats
    high = squares.astype(BF16)
    low = (squares - high.astype(F32)).astype(BF16)
    width = ones.shape[0]
    sums = [
        dot(high[:, i : i + width], ones) + dot(low[:, i : i + width], ones)
        for i in range(0, floats.shape[1], width)
    ]
    mean = jnp.concatenate(sums, axis=1) * (1.0 / channels)
    return floats * lax.rsqrt(mean + 1e-06)


def spread(heads, width, first):
    a = lax.broadcasted_iota(jnp.int32, (128, width), 0)
    b = lax.broadcasted_iota(jnp.int32, (128, width), 1) // (width // heads)
    return jnp.where(a == b + first, 1.0, 0.0).astype(BF16)


def gathered(heads, width, first):
    a = lax.broadcasted_iota(jnp.int32, (width, 128), 0)
    b = lax.broadcasted_iota(jnp.int32, (width, 128), 1) - first
    return jnp.where((a == b * (width // heads)) & (b >= 0) & (b < heads), 1.0, 0.0).astype(BF16)


def latent_kernel(
    scale, place, x, gain, weights, slots, slot_gain, asking, keys, values, mine, other
):
    rows, cols, width = x.shape
    heads = H
    channels = width // heads
    latents = slots.shape[0]
    ones = head_ones(256, channels)
    for i in range(rows // 2):
        tokens = x[2 * i : 2 * i + 2].reshape(2 * cols, width).astype(F32)
        normed = token_norm(tokens, gain[...])
        both = dot(normed, weights[:, width:])
        here = slice(2 * i * cols, (2 * i + 2) * cols)
        keys[here, :] = head_norm(both[:, :width], ones, channels).astype(BF16)
        values[here, :] = both[:, width:].astype(BF16)
    slot_normed = token_norm(slots[...].astype(F32), slot_gain[...])
    asked = head_norm(dot(slot_normed, asking[...]), ones, channels).astype(BF16)
    half = latents // 2
    first = place[4] == 0
    lanes = lax.broadcasted_iota(jnp.int32, (1, 128), 1)
    peaks = jnp.zeros((latents, 128), F32)
    totals = jnp.zeros((latents, 128), F32)
    per = 128 // channels
    for pair in range(heads // per):
        at = slice(pair * 128, (pair + 1) * 128)
        out = jnp.zeros((latents, 128), F32)
        for inner in range(per):
            head = pair * per + inner
            own = (lanes // channels) == inner
            query = asked[:, at] * jnp.where(own, 1.0, 0.0).astype(BF16)
            scores = lax.dot_general(query, keys[:, at], CONTRACT_LAST, preferred_element_type=F32)
            scores = scores * (scale[head] * LOG2E)
            peak = jnp.max(scores, axis=-1, keepdims=True)
            peak = (jnp.ceil(peak * 0.5) * 2.0).astype(BF16).astype(F32)
            expo = jnp.exp2(scores - peak)
            total = jnp.sum(expo, axis=-1, keepdims=True)
            out = jnp.where(own, dot(expo.astype(BF16), values[:, at]), out)
            peaks = jnp.where(lanes == head, peak, peaks)
            totals = jnp.where(lanes == head, total, totals)
        out = out.astype(BF16)
        mine[:, at] = jnp.where(first, out[:half], out[half:])
        other[:, at] = jnp.where(first, out[half:], out[:half])
    high = totals.astype(BF16).astype(F32)
    low = totals - high
    meta = peaks + pltpu.roll(high, heads, 1) + pltpu.roll(low, 2 * heads, 1)
    meta = meta.astype(BF16)
    mine[:, width:] = jnp.where(first, meta[:half], meta[half:])
    other[:, width:] = jnp.where(first, meta[half:], meta[:half])


def opened(part, width):
    meta = part[:, width:]
    peak = dot(meta, spread(H, width, 0))
    total = dot(meta, spread(H, width, H) + spread(H, width, 2 * H))
    return (part[:, :width].astype(F32), peak, total)


def joined(parts, width):
    items = [opened(p, width) for p in parts]
    peak = items[0][1]
    for item in items[1:]:
        peak = jnp.maximum(peak, item[1])
    out, total = (0.0, 0.0)
    for o, m, t in items:
        factor = jnp.exp2(m - peak)
        out = out + o * factor
        total = total + t * factor
    return (out, peak, total)


def join_kernel(a, b, result):
    width = result.shape[1] - 128
    out, peak, total = joined([a[...], b[...]], width)
    result[:, :width] = out.astype(BF16)
    high = total.astype(BF16)
    low = (total - high.astype(F32)).astype(BF16)
    meta = (
        dot(peak.astype(BF16), gathered(H, width, 0))
        + dot(high, gathered(H, width, H))
        + dot(low, gathered(H, width, 2 * H))
    )
    result[:, width:] = meta.astype(BF16)


def last_kernel(a, b, exits, result):
    width = result.shape[1]
    out, _, total = joined([a[...], b[...]], width)
    result[...] = dot((out / total).astype(BF16), exits[...]).astype(BF16)


def windows(tokens, side):
    cols, width = tokens.shape
    own = tokens.reshape(cols // BLK, BLK, width)
    side = side.reshape(1, BLK, width)
    after = jnp.concatenate([own[1:], side], axis=0)
    before = jnp.concatenate([side, own[:-1]], axis=0)
    place = lax.broadcasted_iota(jnp.int32, own.shape, 1)
    rim = jnp.where(place < BLK // 2, after, before)
    return jnp.concatenate([own, rim], axis=1).astype(BF16)


def own_kernel(x, side, gain, weights, keys, values, queries, key_win, value_win):
    rows, cols, width = x.shape
    channels = width // H
    ones = head_ones(256, channels)
    beside = token_norm(side[...].reshape(rows * BLK, width).astype(F32), gain[...])
    both = dot(beside, weights[:, width:])
    side_keys = head_norm(both[:, :width], ones, channels)
    side_values = both[:, width:]
    for i in range(rows // 2):
        tokens = x[2 * i : 2 * i + 2].reshape(2 * cols, width).astype(F32)
        normed = token_norm(tokens, gain[...])
        query = head_norm(dot(normed, weights[:, :width]), ones, channels)
        query = query.reshape(2, cols // BLK, BLK, width).transpose(1, 0, 2, 3)
        queries[:, 16 * i : 16 * i + 16, :] = query.reshape(cols // BLK, 16, width).astype(BF16)
    for r in range(rows):
        here = slice(r * cols, (r + 1) * cols)
        at = slice(r * BLK, (r + 1) * BLK)
        key_win[r] = windows(keys[here, :].astype(F32), side_keys[at])
        value_win[r] = windows(values[here, :].astype(F32), side_values[at])


def halo_kernel(
    scale,
    place,
    x,
    up,
    down,
    up_side,
    down_side,
    gain,
    weights,
    exits,
    queries,
    key_win,
    value_win,
    tokens_out,
    key_rim,
    value_rim,
    attended,
):
    rows, cols, width = x.shape
    channels = width // H
    ones = head_ones(256, channels)
    blocks = cols // BLK
    lines = rows + 2 * RIM

    corner = jnp.concatenate([up_side[...], down_side[...]], axis=0)
    beside = token_norm(corner.reshape(2 * RIM * BLK, width).astype(F32), gain[...])
    both = dot(beside, weights[:, width:])
    side_keys = head_norm(both[:, :width], ones, channels)
    side_values = both[:, width:]
    for n, ref in enumerate((up, down)):
        for r in range(RIM):
            normed = token_norm(ref[r].astype(F32), gain[...])
            both = dot(normed, weights[:, width:])
            line = n * RIM + r
            at = slice(line * BLK, (line + 1) * BLK)
            key_rim[line] = windows(head_norm(both[:, :width], ones, channels), side_keys[at])
            value_rim[line] = windows(both[:, width:], side_values[at])

    spot = lax.broadcasted_iota(jnp.int32, (1, lines * 16), 1)
    line, sub = (spot // 16, spot % 16)
    upper = (line >= rows) & (line < rows + RIM)
    lower = line >= rows + RIM
    fixed = (sub == BLK + RIM) | (sub == BLK + RIM + 1)
    fixed = fixed | (upper & (place[0] == 0)) | (lower & (place[1] == 0))
    right = (sub >= BLK) & (sub < BLK + RIM)
    left = sub >= 2 * BLK - RIM
    group = 256
    per = group // channels
    owner = lax.broadcasted_iota(jnp.int32, (1, group), 1) // channels

    def one_block(block):
        gone = fixed | (right & ((place[3] == 0) & (block == blocks - 1)))
        gone = gone | (left & ((place[2] == 0) & (block == 0)))
        bias = jnp.where(gone, NEG, 0.0)
        outs = []
        for g in range(width // group):
            at = slice(g * group, (g + 1) * group)
            query = queries[block, :, at]
            stacked = jnp.concatenate(
                [query * jnp.where(owner == h, 1.0, 0.0).astype(BF16) for h in range(per)], axis=0
            )
            key = jnp.concatenate(
                [
                    key_win[:, block, :, at].reshape(rows * 16, group),
                    key_rim[:, block, :, at].reshape(2 * RIM * 16, group),
                ],
                axis=0,
            )
            value = jnp.concatenate(
                [
                    value_win[:, block, :, at].reshape(rows * 16, group),
                    value_rim[:, block, :, at].reshape(2 * RIM * 16, group),
                ],
                axis=0,
            )
            scores = lax.dot_general(stacked, key, CONTRACT_LAST, preferred_element_type=F32)
            expos, totals = ([], [])
            n = BLK * BLK
            for h in range(per):
                s = scores[h * n : (h + 1) * n] * (scale[g * per + h] * LOG2E) + bias
                expo = jnp.exp2(s - jnp.max(s, axis=-1, keepdims=True))
                totals.append(jnp.sum(expo, axis=-1, keepdims=True))
                expos.append(expo.astype(BF16))
            mixed = dot(jnp.concatenate(expos, axis=0), value)
            out = jnp.zeros((n, group), F32)
            for h in range(per):
                out = jnp.where(owner == h, mixed[h * n : (h + 1) * n] / totals[h], out)
            outs.append(out)
        return jnp.concatenate(outs, axis=1).reshape(BLK, BLK, width)

    def two_blocks(i, carry):
        pair = jnp.concatenate([one_block(2 * i), one_block(2 * i + 1)], axis=1)
        attended[:, pl.ds(pl.multiple_of(i * 16, 16), 16), :] = pair.astype(BF16)
        return carry

    lax.fori_loop(0, blocks // 2, two_blocks, 0)
    for i in range(rows // 2):
        here = slice(2 * i, 2 * i + 2)
        branch = dot(attended[here].reshape(2 * cols, width), exits[...])
        tokens_out[here] = (x[here].astype(F32) + branch.reshape(2, cols, width)).astype(BF16)


def call(kernel, outs, ins, scratch=(), flops=0, smem=0):
    shapes = [jax.ShapeDtypeStruct(*o) for o in outs]
    moved = sum(math.prod(s.shape) * s.dtype.itemsize for s in shapes + list(ins))
    return pl.pallas_call(
        kernel,
        out_shape=shapes,
        in_specs=[SMEM] * smem + [VMEM] * (len(ins) - smem),
        out_specs=[VMEM] * len(shapes),
        scratch_shapes=list(scratch),
        compiler_params=pltpu.CompilerParams(vmem_limit_bytes=48 * 1024 * 1024),
        cost_estimate=pl.CostEstimate(flops=flops, bytes_accessed=moved, transcendentals=0),
    )(*ins)


def per_device(
    crop_feature_grid,
    pixel_layernorm_gain,
    triple_projection_matrix,
    halo_exit_matrix,
    memory_slots,
    memory_layernorm_gain,
    memory_asking_matrix,
    memory_exit_matrix,
    branch_logit_multiplier,
):
    x = crop_feature_grid
    rows, cols, width = x.shape
    latents = memory_slots.shape[0]
    tall, wide = (lax.axis_size("rows"), lax.axis_size("cols"))
    row, col = (lax.axis_index("rows"), lax.axis_index("cols"))
    place = jnp.stack([row > 0, row < tall - 1, col > 0, col < wide - 1, col > 0])
    place = place.astype(jnp.int32)
    scale = branch_logit_multiplier / math.sqrt(width // H)
    gain = pixel_layernorm_gain.reshape(1, width)
    slot_gain = memory_layernorm_gain.reshape(1, width)

    downward = [(i, i + 1) for i in range(tall - 1)]
    upward = [(i + 1, i) for i in range(tall - 1)]
    swap = [(0, 1), (1, 0)]
    edge = jnp.where(col == 0, x[:, cols - BLK :], x[:, :BLK])
    up = lax.ppermute(x[rows - RIM :], "rows", downward)
    down = lax.ppermute(x[:RIM], "rows", upward)
    side = lax.ppermute(edge, "cols", swap)
    across = [(i * 2 + c, j * 2 + 1 - c) for i, j in downward for c in range(2)]
    back = [(j, i) for i, j in across]
    up_side = lax.ppermute(edge[rows - RIM :], ("rows", "cols"), across)
    down_side = lax.ppermute(edge[:RIM], ("rows", "cols"), back)

    half = latents // 2
    tokens = rows * cols
    keys, values, mine, other = call(
        latent_kernel,
        [
            ((tokens, width), BF16),
            ((tokens, width), BF16),
            ((half, width + 128), BF16),
            ((half, width + 128), BF16),
        ],
        (
            scale,
            place,
            x,
            gain,
            triple_projection_matrix,
            memory_slots,
            slot_gain,
            memory_asking_matrix,
        ),
        flops=4 * 10**9,
        smem=2,
    )
    parts = [mine, lax.ppermute(other, "cols", swap)]
    step = 1
    while step < tall:
        pairs = [(i, i ^ step) for i in range(tall)]
        (whole,) = call(join_kernel, [((half, width + 128), BF16)], parts, flops=10**8)
        parts = [whole, lax.ppermute(whole, "rows", pairs)]
        step *= 2
    (mixed,) = call(
        last_kernel, [((half, width), BF16)], (*parts, memory_exit_matrix), flops=10**8
    )
    theirs = lax.ppermute(mixed, "cols", swap)
    latent_mix = jnp.where(
        col == 0, jnp.concatenate([mixed, theirs]), jnp.concatenate([theirs, mixed])
    )

    blocks = cols // BLK
    queries, key_win, value_win = call(
        own_kernel,
        [
            ((blocks, rows * BLK, width), BF16),
            ((rows, blocks, 16, width), BF16),
            ((rows, blocks, 16, width), BF16),
        ],
        (x, side, gain, triple_projection_matrix, keys, values),
        flops=2 * 10**9,
    )
    (tokens_out,) = call(
        halo_kernel,
        [(x.shape, BF16)],
        (
            scale,
            place,
            x,
            up,
            down,
            up_side,
            down_side,
            gain,
            triple_projection_matrix,
            halo_exit_matrix,
            queries,
            key_win,
            value_win,
        ),
        scratch=[
            pltpu.VMEM((2 * RIM, blocks, 16, width), BF16),
            pltpu.VMEM((2 * RIM, blocks, 16, width), BF16),
            pltpu.VMEM((rows, cols, width), BF16),
        ],
        flops=6 * 10**9,
        smem=2,
    )
    return (tokens_out, latent_mix)


def solution(mesh):
    return jax.shard_map(
        per_device,
        mesh=mesh,
        in_specs=(P(("grp", "rows"), "cols", None), P(), P(), P(), P(), P(), P(), P(), P()),
        out_specs=(P(("grp", "rows"), "cols", None), P("grp", None)),
        check_vma=False,
    )
```

```python
import functools
import math

import jax
import jax.numpy as jnp
from jax import lax
from jax.experimental import pallas as pl
from jax.experimental.pallas import tpu as pltpu
from jax.sharding import PartitionSpec as P

H = 8
BLK = 8
RIM = 3
F32 = jnp.float32
BF16 = jnp.bfloat16
NEG = -1e30
HBM = pl.BlockSpec(memory_space=pltpu.HBM)
VMEM = pl.BlockSpec(memory_space=pltpu.VMEM)
SMEM = pl.BlockSpec(memory_space=pltpu.SMEM)
CONTRACT_LAST = (((1,), (1,)), ((), ()))


def dot(a, b):
    return jnp.dot(a, b, preferred_element_type=F32)


def token_norm(floats, gain):
    scaled = floats * lax.rsqrt(jnp.mean(floats * floats, axis=-1, keepdims=True) + 1e-05)
    return (scaled * gain).astype(BF16)


def head_ones(width, channels):
    a = lax.broadcasted_iota(jnp.int32, (width, width), 0) // channels
    b = lax.broadcasted_iota(jnp.int32, (width, width), 1) // channels
    return jnp.where(a == b, 1.0, 0.0).astype(BF16)


def head_norm(floats, ones, channels):
    squares = floats * floats
    high = squares.astype(BF16)
    low = (squares - high.astype(F32)).astype(BF16)
    width = ones.shape[0]
    sums = [
        dot(high[:, i : i + width], ones) + dot(low[:, i : i + width], ones)
        for i in range(0, floats.shape[1], width)
    ]
    mean = jnp.concatenate(sums, axis=1) * (1.0 / channels)
    return floats * lax.rsqrt(mean + 1e-06)


def latent_kernel(
    scale,
    place,
    x_far,
    gain,
    weights_far,
    slots_far,
    slot_gain,
    asking_far,
    keys,
    values,
    mine,
    other,
    x,
    weights,
    slots,
    asking,
    sems,
):
    rows, cols, width = x.shape
    heads = H
    channels = width // heads
    latents = slots.shape[0]
    copies = [(slots_far, slots), (asking_far, asking)]
    copies += [(weights_far.at[:, width:], weights), (x_far, x)]
    copies = [
        pltpu.make_async_copy(far, near, sems.at[n]) for n, (far, near) in enumerate(copies)
    ]
    for copy in copies:
        copy.start()
    ones = head_ones(256, channels)
    copies[0].wait()
    copies[1].wait()
    slot_normed = token_norm(slots[...].astype(F32), slot_gain[...])
    asked = head_norm(dot(slot_normed, asking[...]), ones, channels).astype(BF16)
    copies[2].wait()
    copies[3].wait()
    for i in range(rows // 2):
        tokens = x[2 * i : 2 * i + 2].reshape(2 * cols, width).astype(F32)
        normed = token_norm(tokens, gain[...])
        both = dot(normed, weights[...])
        here = slice(2 * i * cols, (2 * i + 2) * cols)
        keys[here, :] = head_norm(both[:, :width], ones, channels).astype(BF16)
        values[here, :] = both[:, width:].astype(BF16)
    half = latents // 2
    first = place[4] == 0
    lanes = lax.broadcasted_iota(jnp.int32, (1, 128), 1)
    peaks = jnp.zeros((latents, 128), F32)
    totals = jnp.zeros((latents, 128), F32)
    per = 128 // channels
    for pair in range(heads // per):
        at = slice(pair * 128, (pair + 1) * 128)
        owner = lanes // channels
        query = jnp.concatenate(
            [asked[:, at] * jnp.where(owner == n, 1.0, 0.0).astype(BF16) for n in range(per)],
            axis=0,
        )
        scores = lax.dot_general(query, keys[:, at], CONTRACT_LAST, preferred_element_type=F32)
        expos = []
        for inner in range(per):
            head = pair * per + inner
            score = scores[inner * latents : (inner + 1) * latents] * (scale[head] * (math.log2(math.e) / math.sqrt(channels)))
            peak = jnp.max(score, axis=-1, keepdims=True)
            peak = (jnp.ceil(peak * 0.5) * 2.0).astype(BF16).astype(F32)
            expo = jnp.exp2(score - peak)
            total = jnp.sum(expo, axis=-1, keepdims=True)
            expos.append(expo.astype(BF16))
            peaks = jnp.where(lanes == head, peak, peaks)
            totals = jnp.where(lanes == head, total, totals)
        mixed = dot(jnp.concatenate(expos, axis=0), values[:, at])
        out = mixed[:latents]
        for inner in range(1, per):
            out = jnp.where(owner == inner, mixed[inner * latents : (inner + 1) * latents], out)
        out = out.astype(BF16)
        mine[:half, at] = jnp.where(first, out[:half], out[half:])
        other[:half, at] = jnp.where(first, out[half:], out[:half])
    high = totals.astype(BF16)
    low = (totals - high.astype(F32)).astype(BF16)
    sub = lax.broadcasted_iota(jnp.int32, (16, 128), 0)
    pick = jnp.where(sub == lax.broadcasted_iota(jnp.int32, (16, 128), 1), 1.0, 0.0)
    pick = jnp.where(sub < heads, pick, 0.0).astype(BF16)
    for n, columns in enumerate((peaks.astype(BF16), high, low)):
        flat = lax.dot_general(pick, columns, CONTRACT_LAST, preferred_element_type=F32)
        flat = flat.astype(BF16)
        at = slice(n * half, (n + 1) * half)
        mine[half:, at] = jnp.where(first, flat[:, :half], flat[:, half:])
        other[half:, at] = jnp.where(first, flat[:, half:], flat[:, :half])
    rest = slice(3 * half, width)
    mine[half:, rest] = jnp.zeros((16, width - 3 * half), BF16)
    other[half:, rest] = jnp.zeros((16, width - 3 * half), BF16)


def head_rows(width, all_lanes):
    channels = width // H
    a = lax.broadcasted_iota(jnp.int32, (16, width), 0)
    b = lax.broadcasted_iota(jnp.int32, (16, width), 1)
    same = (b // channels == a) if all_lanes else (b == a * channels)
    return jnp.where(same & (a < H), 1.0, 0.0).astype(BF16)


def opened(part, width):
    half = part.shape[0] - 16
    rows = head_rows(width, True)

    def spread(n):
        return lax.dot_general(
            part[half:, n * half : (n + 1) * half],
            rows,
            (((0,), (0,)), ((), ())),
            preferred_element_type=F32,
        )

    return (part[:half].astype(F32), spread(0), spread(1) + spread(2))


def joined(parts, width):
    items = [opened(p, width) for p in parts]
    peak = items[0][1]
    for item in items[1:]:
        peak = jnp.maximum(peak, item[1])
    out, total = (0.0, 0.0)
    for o, m, t in items:
        factor = jnp.exp2(m - peak)
        out = out + o * factor
        total = total + t * factor
    return (out, peak, total)


def join_kernel(a, b, result):
    width = result.shape[1]
    half = result.shape[0] - 16
    out, peak, total = joined([a[...], b[...]], width)
    result[:half] = out.astype(BF16)
    high = total.astype(BF16)
    low = (total - high.astype(F32)).astype(BF16)
    rows = head_rows(width, False)
    for n, spread in enumerate((peak.astype(BF16), high, low)):
        flat = lax.dot_general(rows, spread, CONTRACT_LAST, preferred_element_type=F32)
        result[half:, n * half : (n + 1) * half] = flat.astype(BF16)
    result[half:, 3 * half :] = jnp.zeros((16, width - 3 * half), BF16)


def last_kernel(a, b, exits, result):
    width = result.shape[1]
    out, _, total = joined([a[...], b[...]], width)
    result[...] = dot((out / total).astype(BF16), exits[...]).astype(BF16)


def windows(tokens, side):
    cols, width = tokens.shape
    own = tokens.reshape(cols // BLK, BLK, width)
    side = side.reshape(1, BLK, width)
    after = jnp.concatenate([own[1:], side], axis=0)
    before = jnp.concatenate([side, own[:-1]], axis=0)
    place = lax.broadcasted_iota(jnp.int32, own.shape, 1)
    rim = jnp.where(place < BLK // 2, after, before)
    return jnp.concatenate([own, rim], axis=1).astype(BF16)


def own_kernel(x, side, gain, weights, keys, values, queries, key_win, value_win):
    rows, cols, width = x.shape
    channels = width // H
    ones = head_ones(256, channels)
    beside = token_norm(side[...].reshape(rows * BLK, width).astype(F32), gain[...])
    both = dot(beside, weights[:, width:])
    side_keys = head_norm(both[:, :width], ones, channels)
    side_values = both[:, width:]
    for i in range(rows // 2):
        tokens = x[2 * i : 2 * i + 2].reshape(2 * cols, width).astype(F32)
        normed = token_norm(tokens, gain[...])
        query = head_norm(dot(normed, weights[:, :width]), ones, channels)
        query = query.reshape(2, cols // BLK, BLK, width).transpose(1, 0, 2, 3)
        queries[:, 16 * i : 16 * i + 16, :] = query.reshape(cols // BLK, 16, width).astype(BF16)
    for r in range(rows):
        here = slice(r * cols, (r + 1) * cols)
        at = slice(r * BLK, (r + 1) * BLK)
        key_win[r] = windows(keys[here, :].astype(F32), side_keys[at])
        value_win[r] = windows(values[here, :].astype(F32), side_values[at])


def rim_kernel(up, down, gain, weights, key_rim, value_rim):
    lines, cols, width = up.shape
    channels = width // H
    ones = head_ones(256, channels)
    for n, ref in enumerate((up, down)):
        normed = token_norm(ref[...].astype(F32).reshape(lines * cols, width), gain[...])
        both = dot(normed, weights[:, width:])
        key = head_norm(both[:, :width], ones, channels)
        value = both[:, width:]
        for r in range(lines):
            at = slice(r * cols, (r + 1) * cols)
            key_rim[n * lines + r] = windows(key[at], key[at.start : at.start + BLK])
            value_rim[n * lines + r] = windows(value[at], value[at.start : at.start + BLK])


def halo_kernel(
    scale,
    place,
    x,
    corner,
    gain,
    weights,
    exits,
    queries,
    key_win,
    value_win,
    key_rim,
    value_rim,
    *refs,
    start,
    stop,
):
    if start == 0:
        attended, key_end, value_end = refs
    else:
        earlier, tokens_out, key_end, value_end, attended = refs
    rows, cols, width = x.shape
    channels = width // H
    ones = head_ones(256, channels)
    blocks = cols // BLK
    lines = rows + 2 * RIM

    normed = token_norm(corner[...].reshape(2 * RIM * BLK, width).astype(F32), gain[...])
    both = dot(normed, weights[:, width:])
    corner_keys = head_norm(both[:, :width], ones, channels).reshape(2 * RIM, BLK, width)
    corner_values = both[:, width:].reshape(2 * RIM, BLK, width)
    sub = lax.broadcasted_iota(jnp.int32, (1, 16, 1), 1)
    for block, beyond in ((0, sub >= 2 * BLK - RIM), (blocks - 1, sub < BLK + RIM)):
        if not start <= block < stop:
            continue
        beyond = beyond & (sub >= BLK)
        for rim, tile, end in (
            (key_rim, corner_keys, key_end),
            (value_rim, corner_values, value_end),
        ):
            double = jnp.concatenate([tile, tile], axis=1)
            kept = rim[:, block].astype(F32)
            end[...] = jnp.where(beyond, double, kept).astype(BF16)

    spot = lax.broadcasted_iota(jnp.int32, (1, lines * 16), 1)
    line, sub = (spot // 16, spot % 16)
    upper = (line >= rows) & (line < rows + RIM)
    lower = line >= rows + RIM
    fixed = (sub == BLK + RIM) | (sub == BLK + RIM + 1)
    fixed = fixed | (upper & (place[0] == 0)) | (lower & (place[1] == 0))
    right = (sub >= BLK) & (sub < BLK + RIM)
    left = sub >= 2 * BLK - RIM
    group = 256
    per = group // channels
    owner = lax.broadcasted_iota(jnp.int32, (1, group), 1) // channels

    def one_block(block):
        gone = fixed
        if block == 0:
            gone = gone | (left & (place[2] == 0))
        if block == blocks - 1:
            gone = gone | (right & (place[3] == 0))
        bias = jnp.where(gone, NEG, 0.0)
        outs = []
        for g in range(width // group):
            at = slice(g * group, (g + 1) * group)

            def around(win, rim, end):
                if block == 0 or block == blocks - 1:
                    far = end[:, :, at]
                else:
                    far = rim[:, block, :, at]
                own = win[:, block, :, at].reshape(rows * 16, group)
                return jnp.concatenate([own, far.reshape(2 * RIM * 16, group)], axis=0)

            query = queries[block, :, at]
            stacked = jnp.concatenate(
                [query * jnp.where(owner == h, 1.0, 0.0).astype(BF16) for h in range(per)], axis=0
            )
            key = around(key_win, key_rim, key_end)
            value = around(value_win, value_rim, value_end)
            scores = lax.dot_general(stacked, key, CONTRACT_LAST, preferred_element_type=F32)
            expos, totals = ([], [])
            n = BLK * BLK
            for h in range(per):
                s = scores[h * n : (h + 1) * n] * (scale[g * per + h] * (math.log2(math.e) / math.sqrt(channels))) + bias
                expo = jnp.exp2(s - jnp.max(s, axis=-1, keepdims=True))
                totals.append(jnp.sum(expo, axis=-1, keepdims=True))
                expos.append(expo.astype(BF16))
            mixed = dot(jnp.concatenate(expos, axis=0), value)
            out = jnp.zeros((n, group), F32)
            for h in range(per):
                out = jnp.where(owner == h, mixed[h * n : (h + 1) * n] / totals[h], out)
            outs.append(out)
        return jnp.concatenate(outs, axis=1).reshape(BLK, BLK, width)

    for i in range((stop - start) // 2):
        block = start + 2 * i
        pair = jnp.concatenate([one_block(block), one_block(block + 1)], axis=1)
        attended[:, 16 * i : 16 * i + 16, :] = pair.astype(BF16)
    if start == 0:
        return
    for part, at in ((earlier, slice(0, start * BLK)), (attended, slice(start * BLK, cols))):
        count = at.stop - at.start
        for i in range(rows // 4):
            here = slice(4 * i, 4 * i + 4)
            branch = dot(part[here].reshape(4 * count, width), exits[...])
            total = x[here, at].astype(F32) + branch.reshape(4, count, width)
            tokens_out[here, at] = total.astype(BF16)


def call(kernel, outs, ins, scratch=(), megabytes=16, smem=0, far=()):
    shapes = [jax.ShapeDtypeStruct(*o) for o in outs]
    return pl.pallas_call(
        kernel,
        out_shape=shapes,
        in_specs=[SMEM if n < smem else HBM if n in far else VMEM for n in range(len(ins))],
        out_specs=[VMEM] * len(shapes),
        scratch_shapes=list(scratch),
        compiler_params=pltpu.CompilerParams(vmem_limit_bytes=megabytes * 1024 * 1024),
        cost_estimate=pl.CostEstimate(flops=1000, bytes_accessed=1000, transcendentals=0),
    )(*ins)


def per_device(
    crop_feature_grid,
    pixel_layernorm_gain,
    triple_projection_matrix,
    halo_exit_matrix,
    memory_slots,
    memory_layernorm_gain,
    memory_asking_matrix,
    memory_exit_matrix,
    branch_logit_multiplier,
):
    x = crop_feature_grid
    rows, cols, width = x.shape
    latents = memory_slots.shape[0]
    tall, wide = (lax.axis_size("rows"), lax.axis_size("cols"))
    row, col = (lax.axis_index("rows"), lax.axis_index("cols"))
    place = jnp.stack([row > 0, row < tall - 1, col > 0, col < wide - 1, col > 0])
    place = place.astype(jnp.int32)
    scale = branch_logit_multiplier
    gain = pixel_layernorm_gain.reshape(1, width)
    slot_gain = memory_layernorm_gain.reshape(1, width)
    weights = triple_projection_matrix

    odd = row % 2 == 1
    near = [(i, i ^ 1) for i in range(tall)]
    far = [(i, j) for i in range(tall) if 0 <= (j := i - 1 if i % 2 == 0 else i + 1) < tall]
    swap = [(0, 1), (1, 0)]

    def edge(array):
        return jnp.where(col == 0, array[:, cols - BLK :], array[:, :BLK])

    top, bottom = (x[:RIM], x[rows - RIM :])
    near_rim = lax.ppermute(jnp.where(odd, top, bottom), "rows", near)
    far_rim = lax.ppermute(jnp.where(odd, bottom, top), "rows", far)
    side = lax.ppermute(edge(x), "cols", swap)
    place, side = lax.optimization_barrier((place, side))

    half = latents // 2
    tokens = rows * cols
    blocks = cols // BLK
    part = ((half + 16, width), BF16)
    keys, values, mine, other = call(
        latent_kernel,
        [((tokens, width), BF16), ((tokens, width), BF16), part, part],
        (scale, place, x, gain, weights, memory_slots, slot_gain, memory_asking_matrix),
        scratch=[
            pltpu.VMEM(x.shape, BF16),
            pltpu.VMEM((width, 2 * width), BF16),
            pltpu.VMEM(memory_slots.shape, BF16),
            pltpu.VMEM(memory_asking_matrix.shape, BF16),
            pltpu.SemaphoreType.DMA((4,)),
        ],
        megabytes=24,
        smem=2,
        far=(2, 4, 5, 7),
    )
    queries, key_win, value_win = call(
        own_kernel,
        [
            ((blocks, rows * BLK, width), BF16),
            ((rows, blocks, 16, width), BF16),
            ((rows, blocks, 16, width), BF16),
        ],
        (x, side, gain, weights, keys, values),
        megabytes=16,
    )
    steps = [2**i for i in range(1, tall.bit_length() - 1)] + [1]
    parts = [mine, lax.ppermute(other, "cols", swap)]
    for n, step in enumerate(steps[:-1]):
        pairs = [(i, i ^ step) for i in range(tall)]
        (whole,) = call(join_kernel, [part], parts, megabytes=4)
        if n == len(steps) - 2:
            whole, near_rim, far_rim, queries = lax.optimization_barrier(
                (whole, near_rim, far_rim, queries)
            )
            up = jnp.where(odd, near_rim, far_rim)
            down = jnp.where(odd, far_rim, near_rim)
            corner = lax.ppermute(jnp.concatenate([edge(up), edge(down)]), "cols", swap)
        parts = [whole, lax.ppermute(whole, "rows", pairs)]

    rim = ((2 * RIM, blocks, 16, width), BF16)
    key_rim, value_rim = call(rim_kernel, [rim, rim], (up, down, gain, weights), megabytes=16)

    def halo(start, stop, outs, earlier, more):
        return call(
            functools.partial(halo_kernel, start=start, stop=stop),
            outs,
            (
                scale,
                place,
                x,
                corner,
                gain,
                weights,
                halo_exit_matrix,
                queries,
                key_win,
                value_win,
                key_rim,
                value_rim,
                *earlier,
            ),
            scratch=[pltpu.VMEM((2 * RIM, 16, width), BF16)] * 2 + more,
            megabytes=24,
            smem=2,
        )[0]

    middle = blocks // 4 * 2
    half_shape = (rows, middle * BLK, width)
    earlier = halo(0, middle, [(half_shape, BF16)], (), [])
    parts[1], earlier = lax.optimization_barrier((parts[1], earlier))
    (whole,) = call(join_kernel, [part], parts, megabytes=4)
    pairs = [(i, i ^ steps[-1]) for i in range(tall)]
    got = lax.ppermute(whole, "rows", pairs)
    rest = (rows, cols - middle * BLK, width)
    tokens_out = halo(middle, blocks, [(x.shape, BF16)], (earlier,), [pltpu.VMEM(rest, BF16)])
    whole, got, tokens_out = lax.optimization_barrier((whole, got, tokens_out))
    (mixed,) = call(
        last_kernel, [((half, width), BF16)], (whole, got, memory_exit_matrix), megabytes=6
    )
    theirs = lax.ppermute(mixed, "cols", swap)
    latent_mix = jnp.where(
        col == 0, jnp.concatenate([mixed, theirs]), jnp.concatenate([theirs, mixed])
    )
    return (tokens_out, latent_mix)


def solution(mesh):
    return jax.shard_map(
        per_device,
        mesh=mesh,
        in_specs=(P(("grp", "rows"), "cols", None), P(), P(), P(), P(), P(), P(), P(), P()),
        out_specs=(P(("grp", "rows"), "cols", None), P("grp", None)),
        check_vma=False,
    )
```

```python
import functools
import math

import jax
import jax.numpy as jnp
from jax import lax
from jax.experimental import pallas as pl
from jax.experimental.pallas import tpu as pltpu
from jax.sharding import PartitionSpec as P

H = 8
BLK = 8
RIM = 3
F32 = jnp.float32
BF16 = jnp.bfloat16
NEG = -1e30
HBM = pl.BlockSpec(memory_space=pltpu.HBM)
VMEM = pl.BlockSpec(memory_space=pltpu.VMEM)
SMEM = pl.BlockSpec(memory_space=pltpu.SMEM)
CONTRACT_LAST = (((1,), (1,)), ((), ()))


def dot(a, b):
    return jnp.dot(a, b, preferred_element_type=F32)


def token_norm(floats, gain):
    scaled = floats * lax.rsqrt(jnp.mean(floats * floats, axis=-1, keepdims=True) + 1e-05)
    return (scaled * gain).astype(BF16)


def head_ones(width, channels):
    a = lax.broadcasted_iota(jnp.int32, (width, width), 0) // channels
    b = lax.broadcasted_iota(jnp.int32, (width, width), 1) // channels
    return jnp.where(a == b, 1.0, 0.0).astype(BF16)


def head_norm(floats, ones, channels):
    squares = floats * floats
    high = squares.astype(BF16)
    low = (squares - high.astype(F32)).astype(BF16)
    width = ones.shape[0]
    sums = [
        dot(high[:, i : i + width], ones) + dot(low[:, i : i + width], ones)
        for i in range(0, floats.shape[1], width)
    ]
    mean = jnp.concatenate(sums, axis=1) * (1.0 / channels)
    return floats * lax.rsqrt(mean + 1e-06)


def latent_kernel(
    scale,
    place,
    x_far,
    gain,
    weights_far,
    slots_far,
    slot_gain,
    asking_far,
    keys,
    values,
    mine,
    other,
    x,
    weights,
    slots,
    asking,
    sems,
):
    rows, cols, width = x.shape
    heads = H
    channels = width // heads
    latents = slots.shape[0]
    copies = [(slots_far, slots), (asking_far, asking)]
    copies += [(weights_far.at[:, width:], weights), (x_far, x)]
    copies = [
        pltpu.make_async_copy(far, near, sems.at[n]) for n, (far, near) in enumerate(copies)
    ]
    for copy in copies:
        copy.start()
    ones = head_ones(256, channels)
    copies[0].wait()
    copies[1].wait()
    slot_normed = token_norm(slots[...].astype(F32), slot_gain[...])
    asked = head_norm(dot(slot_normed, asking[...]), ones, channels).astype(BF16)
    copies[2].wait()
    copies[3].wait()
    for i in range(rows // 2):
        tokens = x[2 * i : 2 * i + 2].reshape(2 * cols, width).astype(F32)
        normed = token_norm(tokens, gain[...])
        both = dot(normed, weights[...])
        here = slice(2 * i * cols, (2 * i + 2) * cols)
        keys[here, :] = head_norm(both[:, :width], ones, channels).astype(BF16)
        values[here, :] = both[:, width:].astype(BF16)
    half = latents // 2
    first = place[4] == 0
    lanes = lax.broadcasted_iota(jnp.int32, (1, 128), 1)
    peaks = jnp.zeros((latents, 128), F32)
    totals = jnp.zeros((latents, 128), F32)
    per = 128 // channels
    for pair in range(heads // per):
        at = slice(pair * 128, (pair + 1) * 128)
        owner = lanes // channels
        query = jnp.concatenate(
            [asked[:, at] * jnp.where(owner == n, 1.0, 0.0).astype(BF16) for n in range(per)],
            axis=0,
        )
        scores = lax.dot_general(query, keys[:, at], CONTRACT_LAST, preferred_element_type=F32)
        expos = []
        for inner in range(per):
            head = pair * per + inner
            score = scores[inner * latents : (inner + 1) * latents] * (scale[head] * (math.log2(math.e) / math.sqrt(channels)))
            peak = jnp.max(score, axis=-1, keepdims=True)
            peak = (jnp.ceil(peak * 0.5) * 2.0).astype(BF16).astype(F32)
            expo = jnp.exp2(score - peak)
            total = jnp.sum(expo, axis=-1, keepdims=True)
            expos.append(expo.astype(BF16))
            peaks = jnp.where(lanes == head, peak, peaks)
            totals = jnp.where(lanes == head, total, totals)
        mixed = dot(jnp.concatenate(expos, axis=0), values[:, at])
        out = mixed[:latents]
        for inner in range(1, per):
            out = jnp.where(owner == inner, mixed[inner * latents : (inner + 1) * latents], out)
        out = out.astype(BF16)
        mine[:half, at] = jnp.where(first, out[:half], out[half:])
        other[:half, at] = jnp.where(first, out[half:], out[:half])
    high = totals.astype(BF16)
    low = (totals - high.astype(F32)).astype(BF16)
    sub = lax.broadcasted_iota(jnp.int32, (16, 128), 0)
    pick = jnp.where(sub == lax.broadcasted_iota(jnp.int32, (16, 128), 1), 1.0, 0.0)
    pick = jnp.where(sub < heads, pick, 0.0).astype(BF16)
    for n, columns in enumerate((peaks.astype(BF16), high, low)):
        flat = lax.dot_general(pick, columns, CONTRACT_LAST, preferred_element_type=F32)
        flat = flat.astype(BF16)
        at = slice(n * half, (n + 1) * half)
        mine[half:, at] = jnp.where(first, flat[:, :half], flat[:, half:])
        other[half:, at] = jnp.where(first, flat[:, half:], flat[:, :half])
    rest = slice(3 * half, width)
    mine[half:, rest] = jnp.zeros((16, width - 3 * half), BF16)
    other[half:, rest] = jnp.zeros((16, width - 3 * half), BF16)


def head_rows(width, all_lanes):
    channels = width // H
    a = lax.broadcasted_iota(jnp.int32, (16, width), 0)
    b = lax.broadcasted_iota(jnp.int32, (16, width), 1)
    same = (b // channels == a) if all_lanes else (b == a * channels)
    return jnp.where(same & (a < H), 1.0, 0.0).astype(BF16)


def opened(part, width):
    half = part.shape[0] - 16
    rows = head_rows(width, True)

    def spread(n):
        return lax.dot_general(
            part[half:, n * half : (n + 1) * half],
            rows,
            (((0,), (0,)), ((), ())),
            preferred_element_type=F32,
        )

    return (part[:half].astype(F32), spread(0), spread(1) + spread(2))


def joined(parts, width):
    items = [opened(p, width) for p in parts]
    peak = items[0][1]
    for item in items[1:]:
        peak = jnp.maximum(peak, item[1])
    out, total = (0.0, 0.0)
    for o, m, t in items:
        factor = jnp.exp2(m - peak)
        out = out + o * factor
        total = total + t * factor
    return (out, peak, total)


def join_kernel(a, b, result):
    width = result.shape[1]
    half = result.shape[0] - 16
    out, peak, total = joined([a[...], b[...]], width)
    result[:half] = out.astype(BF16)
    high = total.astype(BF16)
    low = (total - high.astype(F32)).astype(BF16)
    rows = head_rows(width, False)
    for n, spread in enumerate((peak.astype(BF16), high, low)):
        flat = lax.dot_general(rows, spread, CONTRACT_LAST, preferred_element_type=F32)
        result[half:, n * half : (n + 1) * half] = flat.astype(BF16)
    result[half:, 3 * half :] = jnp.zeros((16, width - 3 * half), BF16)


def last_kernel(a, b, exits, result):
    width = result.shape[1]
    out, _, total = joined([a[...], b[...]], width)
    result[...] = dot((out / total).astype(BF16), exits[...]).astype(BF16)


def windows(tokens, side):
    cols, width = tokens.shape
    own = tokens.reshape(cols // BLK, BLK, width)
    side = side.reshape(1, BLK, width)
    after = jnp.concatenate([own[1:], side], axis=0)
    before = jnp.concatenate([side, own[:-1]], axis=0)
    place = lax.broadcasted_iota(jnp.int32, own.shape, 1)
    rim = jnp.where(place < BLK // 2, after, before)
    return jnp.concatenate([own, rim], axis=1).astype(BF16)


def copy_kernel(a, b):
    b[...] = a[...]


def own_kernel(x, side, gain, weights, keys, values, queries, key_win, value_win):
    rows, cols, width = x.shape
    channels = width // H
    ones = head_ones(256, channels)
    beside = token_norm(side[...].reshape(rows * BLK, width).astype(F32), gain[...])
    both = dot(beside, weights[:, width:])
    side_keys = head_norm(both[:, :width], ones, channels)
    side_values = both[:, width:]
    for i in range(rows // 2):
        tokens = x[2 * i : 2 * i + 2].reshape(2 * cols, width).astype(F32)
        normed = token_norm(tokens, gain[...])
        query = head_norm(dot(normed, weights[:, :width]), ones, channels)
        query = query.reshape(2, cols // BLK, BLK, width).transpose(1, 0, 2, 3)
        queries[:, 16 * i : 16 * i + 16, :] = query.reshape(cols // BLK, 16, width).astype(BF16)
    for r in range(rows):
        here = slice(r * cols, (r + 1) * cols)
        at = slice(r * BLK, (r + 1) * BLK)
        key_win[r] = windows(keys[here, :].astype(F32), side_keys[at])
        value_win[r] = windows(values[here, :].astype(F32), side_values[at])


def rim_kernel(up, down, gain, weights, key_rim, value_rim):
    lines, cols, width = up.shape
    channels = width // H
    ones = head_ones(256, channels)
    for n, ref in enumerate((up, down)):
        normed = token_norm(ref[...].astype(F32).reshape(lines * cols, width), gain[...])
        both = dot(normed, weights[:, width:])
        key = head_norm(both[:, :width], ones, channels)
        value = both[:, width:]
        for r in range(lines):
            at = slice(r * cols, (r + 1) * cols)
            key_rim[n * lines + r] = windows(key[at], key[at.start : at.start + BLK])
            value_rim[n * lines + r] = windows(value[at], value[at.start : at.start + BLK])


def halo_kernel(
    scale,
    place,
    x,
    corner,
    gain,
    weights,
    exits,
    queries,
    key_win,
    value_win,
    key_rim,
    value_rim,
    *refs,
    start,
    stop,
):
    if start == 0:
        attended, key_end, value_end = refs
    else:
        earlier, tokens_out, key_end, value_end, attended = refs
    rows, cols, width = x.shape
    channels = width // H
    ones = head_ones(256, channels)
    blocks = cols // BLK
    lines = rows + 2 * RIM

    normed = token_norm(corner[...].reshape(2 * RIM * BLK, width).astype(F32), gain[...])
    both = dot(normed, weights[:, width:])
    corner_keys = head_norm(both[:, :width], ones, channels).reshape(2 * RIM, BLK, width)
    corner_values = both[:, width:].reshape(2 * RIM, BLK, width)
    sub = lax.broadcasted_iota(jnp.int32, (1, 16, 1), 1)
    for block, beyond in ((0, sub >= 2 * BLK - RIM), (blocks - 1, sub < BLK + RIM)):
        if not start <= block < stop:
            continue
        beyond = beyond & (sub >= BLK)
        for rim, tile, end in (
            (key_rim, corner_keys, key_end),
            (value_rim, corner_values, value_end),
        ):
            double = jnp.concatenate([tile, tile], axis=1)
            kept = rim[:, block].astype(F32)
            end[...] = jnp.where(beyond, double, kept).astype(BF16)

    spot = lax.broadcasted_iota(jnp.int32, (1, lines * 16), 1)
    line, sub = (spot // 16, spot % 16)
    upper = (line >= rows) & (line < rows + RIM)
    lower = line >= rows + RIM
    fixed = (sub == BLK + RIM) | (sub == BLK + RIM + 1)
    fixed = fixed | (upper & (place[0] == 0)) | (lower & (place[1] == 0))
    right = (sub >= BLK) & (sub < BLK + RIM)
    left = sub >= 2 * BLK - RIM
    group = 256
    per = group // channels
    owner = lax.broadcasted_iota(jnp.int32, (1, group), 1) // channels

    def one_block(block):
        gone = fixed
        if block == 0:
            gone = gone | (left & (place[2] == 0))
        if block == blocks - 1:
            gone = gone | (right & (place[3] == 0))
        bias = jnp.where(gone, NEG, 0.0)
        outs = []
        for g in range(width // group):
            at = slice(g * group, (g + 1) * group)

            def around(win, rim, end):
                if block == 0 or block == blocks - 1:
                    far = end[:, :, at]
                else:
                    far = rim[:, block, :, at]
                own = win[:, block, :, at].reshape(rows * 16, group)
                return jnp.concatenate([own, far.reshape(2 * RIM * 16, group)], axis=0)

            query = queries[block, :, at]
            stacked = jnp.concatenate(
                [query * jnp.where(owner == h, 1.0, 0.0).astype(BF16) for h in range(per)], axis=0
            )
            key = around(key_win, key_rim, key_end)
            value = around(value_win, value_rim, value_end)
            scores = lax.dot_general(stacked, key, CONTRACT_LAST, preferred_element_type=F32)
            expos, totals = ([], [])
            n = BLK * BLK
            for h in range(per):
                s = scores[h * n : (h + 1) * n] * (scale[g * per + h] * (math.log2(math.e) / math.sqrt(channels))) + bias
                expo = jnp.exp2(s - jnp.max(s, axis=-1, keepdims=True))
                totals.append(jnp.sum(expo, axis=-1, keepdims=True))
                expos.append(expo.astype(BF16))
            mixed = dot(jnp.concatenate(expos, axis=0), value)
            out = jnp.zeros((n, group), F32)
            for h in range(per):
                out = jnp.where(owner == h, mixed[h * n : (h + 1) * n] / totals[h], out)
            outs.append(out)
        return jnp.concatenate(outs, axis=1).reshape(BLK, BLK, width)

    for i in range((stop - start) // 2):
        block = start + 2 * i
        pair = jnp.concatenate([one_block(block), one_block(block + 1)], axis=1)
        attended[:, 16 * i : 16 * i + 16, :] = pair.astype(BF16)
    if start == 0:
        return
    for part, at in ((earlier, slice(0, start * BLK)), (attended, slice(start * BLK, cols))):
        count = at.stop - at.start
        for i in range(rows // 4):
            here = slice(4 * i, 4 * i + 4)
            branch = dot(part[here].reshape(4 * count, width), exits[...])
            total = x[here, at].astype(F32) + branch.reshape(4, count, width)
            tokens_out[here, at] = total.astype(BF16)


def call(kernel, outs, ins, scratch=(), megabytes=16, smem=0, far=(), flops=1000):
    shapes = [jax.ShapeDtypeStruct(*o) for o in outs]
    return pl.pallas_call(
        kernel,
        out_shape=shapes,
        in_specs=[SMEM if n < smem else HBM if n in far else VMEM for n in range(len(ins))],
        out_specs=[VMEM] * len(shapes),
        scratch_shapes=list(scratch),
        compiler_params=pltpu.CompilerParams(vmem_limit_bytes=megabytes * 1024 * 1024),
        cost_estimate=pl.CostEstimate(flops=flops, bytes_accessed=1000, transcendentals=0),
    )(*ins)


def per_device(
    crop_feature_grid,
    pixel_layernorm_gain,
    triple_projection_matrix,
    halo_exit_matrix,
    memory_slots,
    memory_layernorm_gain,
    memory_asking_matrix,
    memory_exit_matrix,
    branch_logit_multiplier,
):
    x = crop_feature_grid
    rows, cols, width = x.shape
    latents = memory_slots.shape[0]
    tall, wide = (lax.axis_size("rows"), lax.axis_size("cols"))
    row, col = (lax.axis_index("rows"), lax.axis_index("cols"))
    place = jnp.stack([row > 0, row < tall - 1, col > 0, col < wide - 1, col > 0])
    place = place.astype(jnp.int32)
    scale = branch_logit_multiplier
    gain = pixel_layernorm_gain.reshape(1, width)
    slot_gain = memory_layernorm_gain.reshape(1, width)
    weights = triple_projection_matrix

    odd = row % 2 == 1
    near = [(i, i ^ 1) for i in range(tall)]
    far = [(i, j) for i in range(tall) if 0 <= (j := i - 1 if i % 2 == 0 else i + 1) < tall]
    swap = [(0, 1), (1, 0)]

    def edge(array):
        return jnp.where(col == 0, array[:, cols - BLK :], array[:, :BLK])

    top, bottom = (x[:RIM], x[rows - RIM :])
    near_rim = lax.ppermute(jnp.where(odd, top, bottom), "rows", near)
    far_rim = lax.ppermute(jnp.where(odd, bottom, top), "rows", far)
    (side,) = call(copy_kernel, [((rows, BLK, width), BF16)], (edge(x),), megabytes=2, flops=10**10)
    side = lax.ppermute(side, "cols", swap)
    place, side = lax.optimization_barrier((place, side))

    half = latents // 2
    tokens = rows * cols
    blocks = cols // BLK
    part = ((half + 16, width), BF16)
    keys, values, mine, other = call(
        latent_kernel,
        [((tokens, width), BF16), ((tokens, width), BF16), part, part],
        (scale, place, x, gain, weights, memory_slots, slot_gain, memory_asking_matrix),
        scratch=[
            pltpu.VMEM(x.shape, BF16),
            pltpu.VMEM((width, 2 * width), BF16),
            pltpu.VMEM(memory_slots.shape, BF16),
            pltpu.VMEM(memory_asking_matrix.shape, BF16),
            pltpu.SemaphoreType.DMA((4,)),
        ],
        megabytes=24,
        smem=2,
        far=(2, 4, 5, 7),
    )
    queries, key_win, value_win = call(
        own_kernel,
        [
            ((blocks, rows * BLK, width), BF16),
            ((rows, blocks, 16, width), BF16),
            ((rows, blocks, 16, width), BF16),
        ],
        (x, side, gain, weights, keys, values),
        megabytes=16,
    )
    steps = [2**i for i in range(1, tall.bit_length() - 1)] + [1]
    parts = [mine, lax.ppermute(other, "cols", swap)]
    for n, step in enumerate(steps[:-1]):
        pairs = [(i, i ^ step) for i in range(tall)]
        (whole,) = call(join_kernel, [part], parts, megabytes=4)
        if n == len(steps) - 2:
            whole, near_rim, far_rim, queries = lax.optimization_barrier(
                (whole, near_rim, far_rim, queries)
            )
            up = jnp.where(odd, near_rim, far_rim)
            down = jnp.where(odd, far_rim, near_rim)
            corner = lax.ppermute(jnp.concatenate([edge(up), edge(down)]), "cols", swap)
        parts = [whole, lax.ppermute(whole, "rows", pairs)]

    rim = ((2 * RIM, blocks, 16, width), BF16)
    key_rim, value_rim = call(rim_kernel, [rim, rim], (up, down, gain, weights), megabytes=16)

    def halo(start, stop, outs, earlier, more):
        return call(
            functools.partial(halo_kernel, start=start, stop=stop),
            outs,
            (
                scale,
                place,
                x,
                corner,
                gain,
                weights,
                halo_exit_matrix,
                queries,
                key_win,
                value_win,
                key_rim,
                value_rim,
                *earlier,
            ),
            scratch=[pltpu.VMEM((2 * RIM, 16, width), BF16)] * 2 + more,
            megabytes=24,
            smem=2,
        )[0]

    middle = blocks // 4 * 2
    half_shape = (rows, middle * BLK, width)
    earlier = halo(0, middle, [(half_shape, BF16)], (), [])
    parts[1], earlier = lax.optimization_barrier((parts[1], earlier))
    (whole,) = call(join_kernel, [part], parts, megabytes=4)
    pairs = [(i, i ^ steps[-1]) for i in range(tall)]
    got = lax.ppermute(whole, "rows", pairs)
    rest = (rows, cols - middle * BLK, width)
    tokens_out = halo(middle, blocks, [(x.shape, BF16)], (earlier,), [pltpu.VMEM(rest, BF16)])
    whole, got, tokens_out = lax.optimization_barrier((whole, got, tokens_out))
    (mixed,) = call(
        last_kernel, [((half, width), BF16)], (whole, got, memory_exit_matrix), megabytes=6
    )
    theirs = lax.ppermute(mixed, "cols", swap)
    latent_mix = jnp.where(
        col == 0, jnp.concatenate([mixed, theirs]), jnp.concatenate([theirs, mixed])
    )
    return (tokens_out, latent_mix)


def solution(mesh):
    return jax.shard_map(
        per_device,
        mesh=mesh,
        in_specs=(P(("grp", "rows"), "cols", None), P(), P(), P(), P(), P(), P(), P(), P()),
        out_specs=(P(("grp", "rows"), "cols", None), P("grp", None)),
        check_vma=False,
    )
```

```python
import functools
import math

import jax
import jax.numpy as jnp
from jax import lax
from jax.experimental import pallas as pl
from jax.experimental.pallas import tpu as pltpu
from jax.sharding import PartitionSpec as P

H = 8
BLK = 8
RIM = 3
F32 = jnp.float32
BF16 = jnp.bfloat16
NEG = -1e30
HBM = pl.BlockSpec(memory_space=pltpu.HBM)
VMEM = pl.BlockSpec(memory_space=pltpu.VMEM)
SMEM = pl.BlockSpec(memory_space=pltpu.SMEM)
CONTRACT_LAST = (((1,), (1,)), ((), ()))


def dot(a, b):
    return jnp.dot(a, b, preferred_element_type=F32)


def token_norm(floats, gain):
    scaled = floats * lax.rsqrt(jnp.mean(floats * floats, axis=-1, keepdims=True) + 1e-05)
    return (scaled * gain).astype(BF16)


def head_ones(width, channels):
    a = lax.broadcasted_iota(jnp.int32, (width, width), 0) // channels
    b = lax.broadcasted_iota(jnp.int32, (width, width), 1) // channels
    return jnp.where(a == b, 1.0, 0.0).astype(BF16)


def head_norm(floats, ones, channels):
    squares = floats * floats
    high = squares.astype(BF16)
    low = (squares - high.astype(F32)).astype(BF16)
    width = ones.shape[0]
    sums = [
        dot(high[:, i : i + width], ones) + dot(low[:, i : i + width], ones)
        for i in range(0, floats.shape[1], width)
    ]
    mean = jnp.concatenate(sums, axis=1) * (1.0 / channels)
    return floats * lax.rsqrt(mean + 1e-06)


def latent_kernel(
    scale, place, x, gain, weights, slots, slot_gain, asking, keys, values, mine, other
):
    rows, cols, width = x.shape
    heads = H
    channels = width // heads
    latents = slots.shape[0]
    ones = head_ones(256, channels)
    slot_normed = token_norm(slots[...].astype(F32), slot_gain[...])
    asked = head_norm(dot(slot_normed, asking[...]), ones, channels).astype(BF16)
    for i in range(rows // 2):
        tokens = x[2 * i : 2 * i + 2].reshape(2 * cols, width).astype(F32)
        normed = token_norm(tokens, gain[...])
        both = dot(normed, weights[:, width:])
        here = slice(2 * i * cols, (2 * i + 2) * cols)
        keys[here, :] = head_norm(both[:, :width], ones, channels).astype(BF16)
        values[here, :] = both[:, width:].astype(BF16)
    half = latents // 2
    first = place[4] == 0
    lanes = lax.broadcasted_iota(jnp.int32, (1, 128), 1)
    peaks = jnp.zeros((latents, 128), F32)
    totals = jnp.zeros((latents, 128), F32)
    per = 128 // channels
    for pair in range(heads // per):
        at = slice(pair * 128, (pair + 1) * 128)
        owner = lanes // channels
        query = jnp.concatenate(
            [asked[:, at] * jnp.where(owner == n, 1.0, 0.0).astype(BF16) for n in range(per)],
            axis=0,
        )
        scores = lax.dot_general(query, keys[:, at], CONTRACT_LAST, preferred_element_type=F32)
        expos = []
        for inner in range(per):
            head = pair * per + inner
            score = scores[inner * latents : (inner + 1) * latents] * (scale[head] * (math.log2(math.e) / math.sqrt(channels)))
            peak = jnp.max(score, axis=-1, keepdims=True)
            peak = (jnp.ceil(peak * 0.5) * 2.0).astype(BF16).astype(F32)
            expo = jnp.exp2(score - peak)
            total = jnp.sum(expo, axis=-1, keepdims=True)
            expos.append(expo.astype(BF16))
            peaks = jnp.where(lanes == head, peak, peaks)
            totals = jnp.where(lanes == head, total, totals)
        mixed = dot(jnp.concatenate(expos, axis=0), values[:, at])
        out = mixed[:latents]
        for inner in range(1, per):
            out = jnp.where(owner == inner, mixed[inner * latents : (inner + 1) * latents], out)
        out = out.astype(BF16)
        mine[:half, at] = jnp.where(first, out[:half], out[half:])
        other[:half, at] = jnp.where(first, out[half:], out[:half])
    high = totals.astype(BF16)
    low = (totals - high.astype(F32)).astype(BF16)
    sub = lax.broadcasted_iota(jnp.int32, (16, 128), 0)
    pick = jnp.where(sub == lax.broadcasted_iota(jnp.int32, (16, 128), 1), 1.0, 0.0)
    pick = jnp.where(sub < heads, pick, 0.0).astype(BF16)
    for n, columns in enumerate((peaks.astype(BF16), high, low)):
        flat = lax.dot_general(pick, columns, CONTRACT_LAST, preferred_element_type=F32)
        flat = flat.astype(BF16)
        at = slice(n * half, (n + 1) * half)
        mine[half:, at] = jnp.where(first, flat[:, :half], flat[:, half:])
        other[half:, at] = jnp.where(first, flat[:, half:], flat[:, :half])
    rest = slice(3 * half, width)
    mine[half:, rest] = jnp.zeros((16, width - 3 * half), BF16)
    other[half:, rest] = jnp.zeros((16, width - 3 * half), BF16)


def head_rows(width, all_lanes):
    channels = width // H
    a = lax.broadcasted_iota(jnp.int32, (16, width), 0)
    b = lax.broadcasted_iota(jnp.int32, (16, width), 1)
    same = (b // channels == a) if all_lanes else (b == a * channels)
    return jnp.where(same & (a < H), 1.0, 0.0).astype(BF16)


def opened(part, width):
    half = part.shape[0] - 16
    rows = head_rows(width, True)

    def spread(n):
        return lax.dot_general(
            part[half:, n * half : (n + 1) * half],
            rows,
            (((0,), (0,)), ((), ())),
            preferred_element_type=F32,
        )

    return (part[:half].astype(F32), spread(0), spread(1) + spread(2))


def joined(parts, width):
    items = [opened(p, width) for p in parts]
    peak = items[0][1]
    for item in items[1:]:
        peak = jnp.maximum(peak, item[1])
    out, total = (0.0, 0.0)
    for o, m, t in items:
        factor = jnp.exp2(m - peak)
        out = out + o * factor
        total = total + t * factor
    return (out, peak, total)


def join_kernel(a, b, result):
    width = result.shape[1]
    half = result.shape[0] - 16
    out, peak, total = joined([a[...], b[...]], width)
    result[:half] = out.astype(BF16)
    high = total.astype(BF16)
    low = (total - high.astype(F32)).astype(BF16)
    rows = head_rows(width, False)
    for n, spread in enumerate((peak.astype(BF16), high, low)):
        flat = lax.dot_general(rows, spread, CONTRACT_LAST, preferred_element_type=F32)
        result[half:, n * half : (n + 1) * half] = flat.astype(BF16)
    result[half:, 3 * half :] = jnp.zeros((16, width - 3 * half), BF16)


def last_kernel(a, b, exits, result):
    width = result.shape[1]
    out, _, total = joined([a[...], b[...]], width)
    result[...] = dot((out / total).astype(BF16), exits[...]).astype(BF16)


def windows(tokens, side):
    cols, width = tokens.shape
    own = tokens.reshape(cols // BLK, BLK, width)
    side = side.reshape(1, BLK, width)
    after = jnp.concatenate([own[1:], side], axis=0)
    before = jnp.concatenate([side, own[:-1]], axis=0)
    place = lax.broadcasted_iota(jnp.int32, own.shape, 1)
    rim = jnp.where(place < BLK // 2, after, before)
    return jnp.concatenate([own, rim], axis=1).astype(BF16)


def copy_kernel(a, b):
    b[...] = a[...]


def own_kernel(x, side, gain, weights, keys, values, queries, key_win, value_win):
    rows, cols, width = x.shape
    channels = width // H
    ones = head_ones(256, channels)
    beside = token_norm(side[...].reshape(rows * BLK, width).astype(F32), gain[...])
    both = dot(beside, weights[:, width:])
    side_keys = head_norm(both[:, :width], ones, channels)
    side_values = both[:, width:]
    for i in range(rows // 2):
        tokens = x[2 * i : 2 * i + 2].reshape(2 * cols, width).astype(F32)
        normed = token_norm(tokens, gain[...])
        query = head_norm(dot(normed, weights[:, :width]), ones, channels)
        query = query.reshape(2, cols // BLK, BLK, width).transpose(1, 0, 2, 3)
        queries[:, 16 * i : 16 * i + 16, :] = query.reshape(cols // BLK, 16, width).astype(BF16)
    for r in range(rows):
        here = slice(r * cols, (r + 1) * cols)
        at = slice(r * BLK, (r + 1) * BLK)
        key_win[r] = windows(keys[here, :].astype(F32), side_keys[at])
        value_win[r] = windows(values[here, :].astype(F32), side_values[at])


def rim_kernel(up, down, gain, weights, key_rim, value_rim):
    lines, cols, width = up.shape
    channels = width // H
    ones = head_ones(256, channels)
    for n, ref in enumerate((up, down)):
        normed = token_norm(ref[...].astype(F32).reshape(lines * cols, width), gain[...])
        both = dot(normed, weights[:, width:])
        key = head_norm(both[:, :width], ones, channels)
        value = both[:, width:]
        for r in range(lines):
            at = slice(r * cols, (r + 1) * cols)
            key_rim[n * lines + r] = windows(key[at], key[at.start : at.start + BLK])
            value_rim[n * lines + r] = windows(value[at], value[at.start : at.start + BLK])


def halo_kernel(
    scale, place, x, corner, gain, weights, exits, queries, key_win, value_win, key_rim, value_rim,
    *refs, parts, stage
):
    rows, cols, width = x.shape
    channels = width // H
    ones = head_ones(256, channels)
    blocks = cols // BLK
    lines = rows + 2 * RIM
    order = parts[stage]
    if stage == 0:
        (attended,), key_end, value_end = (refs, None, None)
    else:
        first, attended, first_out, key_end, value_end = refs
        start = BLK * parts[0][0]
        count = BLK * len(parts[0])
        for i in range(rows // 4):
            here = slice(4 * i, 4 * i + 4)
            branch = dot(first[here].reshape(4 * count, width), exits[...])
            total = x[here, start : start + count].astype(F32) + branch.reshape(4, count, width)
            first_out[here] = total.astype(BF16)

        normed = token_norm(corner[...].reshape(2 * RIM * BLK, width).astype(F32), gain[...])
        both = dot(normed, weights[:, width:])
        corner_keys = head_norm(both[:, :width], ones, channels).reshape(2 * RIM, BLK, width)
        corner_values = both[:, width:].reshape(2 * RIM, BLK, width)
        sub = lax.broadcasted_iota(jnp.int32, (1, 16, 1), 1)
        for n, (block, beyond) in enumerate(
            ((0, sub >= 2 * BLK - RIM), (blocks - 1, sub < BLK + RIM))
        ):
            beyond = beyond & (sub >= BLK)
            for rim, tile, end in (
                (key_rim, corner_keys, key_end),
                (value_rim, corner_values, value_end),
            ):
                double = jnp.concatenate([tile, tile], axis=1)
                kept = rim[:, block].astype(F32)
                end[n] = jnp.where(beyond, double, kept).astype(BF16)

    spot = lax.broadcasted_iota(jnp.int32, (1, lines * 16), 1)
    line, sub = (spot // 16, spot % 16)
    upper = (line >= rows) & (line < rows + RIM)
    lower = line >= rows + RIM
    fixed = (sub == BLK + RIM) | (sub == BLK + RIM + 1)
    fixed = fixed | (upper & (place[0] == 0)) | (lower & (place[1] == 0))
    right = (sub >= BLK) & (sub < BLK + RIM)
    left = sub >= 2 * BLK - RIM
    group = 256
    per = group // channels
    owner = lax.broadcasted_iota(jnp.int32, (1, group), 1) // channels

    def one_block(block):
        gone = fixed
        if block == 0:
            gone = gone | (left & (place[2] == 0))
        if block == blocks - 1:
            gone = gone | (right & (place[3] == 0))
        bias = jnp.where(gone, NEG, 0.0)
        outs = []
        for g in range(width // group):
            at = slice(g * group, (g + 1) * group)

            def around(win, rim, end):
                if block == 0 or block == blocks - 1:
                    far = end[min(block, 1), :, :, at]
                else:
                    far = rim[:, block, :, at]
                own = win[:, block, :, at].reshape(rows * 16, group)
                return jnp.concatenate([own, far.reshape(2 * RIM * 16, group)], axis=0)

            query = queries[block, :, at]
            stacked = jnp.concatenate(
                [query * jnp.where(owner == h, 1.0, 0.0).astype(BF16) for h in range(per)], axis=0
            )
            key = around(key_win, key_rim, key_end)
            value = around(value_win, value_rim, value_end)
            scores = lax.dot_general(stacked, key, CONTRACT_LAST, preferred_element_type=F32)
            expos, totals = ([], [])
            n = BLK * BLK
            for h in range(per):
                s = scores[h * n : (h + 1) * n] * (scale[g * per + h] * (math.log2(math.e) / math.sqrt(channels))) + bias
                expo = jnp.exp2(s - jnp.max(s, axis=-1, keepdims=True))
                totals.append(jnp.sum(expo, axis=-1, keepdims=True))
                expos.append(expo.astype(BF16))
            mixed = dot(jnp.concatenate(expos, axis=0), value)
            out = jnp.zeros((n, group), F32)
            for h in range(per):
                out = jnp.where(owner == h, mixed[h * n : (h + 1) * n] / totals[h], out)
            outs.append(out)
        return jnp.concatenate(outs, axis=1).reshape(BLK, BLK, width)

    for i in range(len(order) // 2):
        pair = jnp.concatenate([one_block(order[2 * i]), one_block(order[2 * i + 1])], axis=1)
        attended[:, 16 * i : 16 * i + 16, :] = pair.astype(BF16)


def leave_kernel(x, exits, first, second, tokens_out, total, sems):
    rows, cols, width = x.shape
    count = second.shape[1] // 2
    middle = slice(count, cols - count)
    copies = [pltpu.make_async_copy(first, tokens_out.at[:, middle], sems.at[0])]
    copies[0].start()
    for i in range(rows // 4):
        here = slice(4 * i, 4 * i + 4)
        branch = dot(second[here].reshape(8 * count, width), exits[...])
        branch = branch.reshape(4, 2 * count, width)
        for n, at in enumerate((slice(0, count), slice(cols - count, cols))):
            from_x = x[here, at].astype(F32)
            total[here, n * count : (n + 1) * count] = (
                from_x + branch[:, n * count : (n + 1) * count]
            ).astype(BF16)
            copy = pltpu.make_async_copy(
                total.at[here, n * count : (n + 1) * count],
                tokens_out.at[here, at],
                sems.at[len(copies)],
            )
            copy.start()
            copies.append(copy)
    for copy in copies:
        copy.wait()


def call(kernel, outs, ins, scratch=(), megabytes=16, smem=0, far_outs=(), flops=1000):
    shapes = [jax.ShapeDtypeStruct(*o) for o in outs]
    return pl.pallas_call(
        kernel,
        out_shape=shapes,
        in_specs=[SMEM] * smem + [VMEM] * (len(ins) - smem),
        out_specs=[HBM if n in far_outs else VMEM for n in range(len(outs))],
        scratch_shapes=list(scratch),
        compiler_params=pltpu.CompilerParams(vmem_limit_bytes=megabytes * 1024 * 1024),
        cost_estimate=pl.CostEstimate(flops=flops, bytes_accessed=1000, transcendentals=0),
    )(*ins)


def per_device(
    crop_feature_grid,
    pixel_layernorm_gain,
    triple_projection_matrix,
    halo_exit_matrix,
    memory_slots,
    memory_layernorm_gain,
    memory_asking_matrix,
    memory_exit_matrix,
    branch_logit_multiplier,
):
    x = crop_feature_grid
    rows, cols, width = x.shape
    latents = memory_slots.shape[0]
    tall, wide = (lax.axis_size("rows"), lax.axis_size("cols"))
    row, col = (lax.axis_index("rows"), lax.axis_index("cols"))
    odd = row % 2 == 1
    place = jnp.stack([row > 0, row < tall - 1, col > 0, col < wide - 1, col > 0, odd])
    place = place.astype(jnp.int32)
    scale = branch_logit_multiplier
    gain = pixel_layernorm_gain.reshape(1, width)
    slot_gain = memory_layernorm_gain.reshape(1, width)
    weights = triple_projection_matrix

    near = [(i, i ^ 1) for i in range(tall)]
    far = [(i, j) for i in range(tall) if 0 <= (j := i - 1 if i % 2 == 0 else i + 1) < tall]
    swap = [(0, 1), (1, 0)]

    def edge(array):
        return jnp.where(col == 0, array[:, cols - BLK :], array[:, :BLK])

    top, bottom = (x[:RIM], x[rows - RIM :])
    near_rim = lax.ppermute(jnp.where(odd, top, bottom), "rows", near)
    far_rim = lax.ppermute(jnp.where(odd, bottom, top), "rows", far)
    (side,) = call(copy_kernel, [((rows, BLK, width), BF16)], (edge(x),), megabytes=2, flops=10**10)
    side = lax.ppermute(side, "cols", swap)
    place, side = lax.optimization_barrier((place, side))

    half = latents // 2
    tokens = rows * cols
    blocks = cols // BLK
    part = ((half + 16, width), BF16)
    keys, values, mine, other = call(
        latent_kernel,
        [((tokens, width), BF16), ((tokens, width), BF16), part, part],
        (scale, place, x, gain, weights, memory_slots, slot_gain, memory_asking_matrix),
        megabytes=24,
        smem=2,
    )
    queries, key_win, value_win = call(
        own_kernel,
        [
            ((blocks, rows * BLK, width), BF16),
            ((rows, blocks, 16, width), BF16),
            ((rows, blocks, 16, width), BF16),
        ],
        (x, side, gain, weights, keys, values),
        megabytes=16,
    )
    steps = [2**i for i in range(1, tall.bit_length() - 1)] + [1]
    parts = [mine, lax.ppermute(other, "cols", swap)]
    for n, step in enumerate(steps[:-1]):
        pairs = [(i, i ^ step) for i in range(tall)]
        (whole,) = call(join_kernel, [part], parts, megabytes=4)
        if n == len(steps) - 2:
            whole, near_rim, far_rim, queries = lax.optimization_barrier(
                (whole, near_rim, far_rim, queries)
            )
            up = jnp.where(odd, near_rim, far_rim)
            down = jnp.where(odd, far_rim, near_rim)
            corner = lax.ppermute(jnp.concatenate([edge(up), edge(down)]), "cols", swap)
        parts = [whole, lax.ppermute(whole, "rows", pairs)]

    rim = ((2 * RIM, blocks, 16, width), BF16)
    key_rim, value_rim = call(rim_kernel, [rim, rim], (up, down, gain, weights), megabytes=16)
    rest = blocks // 4
    parts_of = (
        list(range(rest, blocks - rest)),
        list(range(rest)) + list(range(blocks - rest, blocks)),
    )

    def halo(stage, outs, earlier=()):
        return call(
            functools.partial(halo_kernel, parts=parts_of, stage=stage),
            [(shape, BF16) for shape in outs],
            (
                scale,
                place,
                x,
                corner if stage else gain,
                gain,
                weights,
                halo_exit_matrix,
                queries,
                key_win,
                value_win,
                key_rim,
                value_rim,
                *earlier,
            ),
            scratch=[pltpu.VMEM((2, 2 * RIM, 16, width), BF16)] * (2 * stage),
            megabytes=24,
            smem=2,
        )

    inner = (rows, cols - 2 * rest * BLK, width)
    outer = (rows, 2 * rest * BLK, width)
    (first,) = halo(0, [inner])
    parts[1], first, corner = lax.optimization_barrier((parts[1], first, corner))
    (whole,) = call(join_kernel, [part], parts, megabytes=4)
    pairs = [(i, i ^ steps[-1]) for i in range(tall)]
    got = lax.ppermute(whole, "rows", pairs)
    second, first = halo(1, [outer, inner], (first,))
    got, second = lax.optimization_barrier((got, second))
    (mixed,) = call(
        last_kernel, [((half, width), BF16)], (whole, got, memory_exit_matrix), megabytes=6
    )
    (tokens_out,) = call(
        leave_kernel,
        [(x.shape, BF16)],
        (x, halo_exit_matrix, first, second),
        scratch=[
            pltpu.VMEM(outer, BF16),
            pltpu.SemaphoreType.DMA((1 + rows // 2,)),
        ],
        megabytes=12,
        far_outs=(0,),
    )
    theirs = lax.ppermute(mixed, "cols", swap)
    theirs, tokens_out = lax.optimization_barrier((theirs, tokens_out))
    latent_mix = jnp.where(
        col == 0, jnp.concatenate([mixed, theirs]), jnp.concatenate([theirs, mixed])
    )
    return (tokens_out, latent_mix)


def solution(mesh):
    return jax.shard_map(
        per_device,
        mesh=mesh,
        in_specs=(P(("grp", "rows"), "cols", None), P(), P(), P(), P(), P(), P(), P(), P()),
        out_specs=(P(("grp", "rows"), "cols", None), P("grp", None)),
        check_vma=False,
    )
```

```python
import functools
import math

import jax
import jax.numpy as jnp
from jax import lax
from jax.experimental import pallas as pl
from jax.experimental.pallas import tpu as pltpu
from jax.sharding import PartitionSpec as P

H = 8
BLK = 8
RIM = 3
F32 = jnp.float32
BF16 = jnp.bfloat16
NEG = -1e30
HBM = pl.BlockSpec(memory_space=pltpu.HBM)
VMEM = pl.BlockSpec(memory_space=pltpu.VMEM)
SMEM = pl.BlockSpec(memory_space=pltpu.SMEM)
CONTRACT_LAST = (((1,), (1,)), ((), ()))


def dot(a, b):
    return jnp.dot(a, b, preferred_element_type=F32)


def token_norm(floats, gain):
    scaled = floats * lax.rsqrt(jnp.mean(floats * floats, axis=-1, keepdims=True) + 1e-05)
    return (scaled * gain).astype(BF16)


def head_ones(width, channels):
    a = lax.broadcasted_iota(jnp.int32, (width, width), 0) // channels
    b = lax.broadcasted_iota(jnp.int32, (width, width), 1) // channels
    return jnp.where(a == b, 1.0, 0.0).astype(BF16)


def head_norm(floats, ones, channels):
    squares = floats * floats
    high = squares.astype(BF16)
    low = (squares - high.astype(F32)).astype(BF16)
    width = ones.shape[0]
    sums = [
        dot(high[:, i : i + width], ones) + dot(low[:, i : i + width], ones)
        for i in range(0, floats.shape[1], width)
    ]
    mean = jnp.concatenate(sums, axis=1) * (1.0 / channels)
    return floats * lax.rsqrt(mean + 1e-06)


def latent_kernel(
    scale, place, x, gain, weights, slots, slot_gain, asking, keys, values, mine, other
):
    rows, cols, width = x.shape
    heads = H
    channels = width // heads
    latents = slots.shape[0]
    ones = head_ones(256, channels)
    slot_normed = token_norm(slots[...].astype(F32), slot_gain[...])
    asked = head_norm(dot(slot_normed, asking[...]), ones, channels).astype(BF16)
    for i in range(rows // 2):
        tokens = x[2 * i : 2 * i + 2].reshape(2 * cols, width).astype(F32)
        normed = token_norm(tokens, gain[...])
        both = dot(normed, weights[:, width:])
        here = slice(2 * i * cols, (2 * i + 2) * cols)
        keys[here, :] = head_norm(both[:, :width], ones, channels).astype(BF16)
        values[here, :] = both[:, width:].astype(BF16)
    half = latents // 2
    first = place[4] == 0
    lanes = lax.broadcasted_iota(jnp.int32, (1, 128), 1)
    peaks = jnp.zeros((latents, 128), F32)
    totals = jnp.zeros((latents, 128), F32)
    per = 128 // channels
    for pair in range(heads // per):
        at = slice(pair * 128, (pair + 1) * 128)
        owner = lanes // channels
        query = jnp.concatenate(
            [asked[:, at] * jnp.where(owner == n, 1.0, 0.0).astype(BF16) for n in range(per)],
            axis=0,
        )
        scores = lax.dot_general(query, keys[:, at], CONTRACT_LAST, preferred_element_type=F32)
        expos = []
        for inner in range(per):
            head = pair * per + inner
            score = scores[inner * latents : (inner + 1) * latents] * (scale[head] * (math.log2(math.e) / math.sqrt(channels)))
            peak = jnp.max(score, axis=-1, keepdims=True)
            peak = (jnp.ceil(peak * 0.5) * 2.0).astype(BF16).astype(F32)
            expo = jnp.exp2(score - peak)
            total = jnp.sum(expo, axis=-1, keepdims=True)
            expos.append(expo.astype(BF16))
            peaks = jnp.where(lanes == head, peak, peaks)
            totals = jnp.where(lanes == head, total, totals)
        mixed = dot(jnp.concatenate(expos, axis=0), values[:, at])
        out = mixed[:latents]
        for inner in range(1, per):
            out = jnp.where(owner == inner, mixed[inner * latents : (inner + 1) * latents], out)
        out = out.astype(BF16)
        mine[:half, at] = jnp.where(first, out[:half], out[half:])
        other[:half, at] = jnp.where(first, out[half:], out[:half])
    high = totals.astype(BF16)
    low = (totals - high.astype(F32)).astype(BF16)
    sub = lax.broadcasted_iota(jnp.int32, (16, 128), 0)
    pick = jnp.where(sub == lax.broadcasted_iota(jnp.int32, (16, 128), 1), 1.0, 0.0)
    pick = jnp.where(sub < heads, pick, 0.0).astype(BF16)
    for n, columns in enumerate((peaks.astype(BF16), high, low)):
        flat = lax.dot_general(pick, columns, CONTRACT_LAST, preferred_element_type=F32)
        flat = flat.astype(BF16)
        at = slice(n * half, (n + 1) * half)
        mine[half:, at] = jnp.where(first, flat[:, :half], flat[:, half:])
        other[half:, at] = jnp.where(first, flat[:, half:], flat[:, :half])
    rest = slice(3 * half, width)
    mine[half:, rest] = jnp.zeros((16, width - 3 * half), BF16)
    other[half:, rest] = jnp.zeros((16, width - 3 * half), BF16)


def head_rows(width, all_lanes):
    channels = width // H
    a = lax.broadcasted_iota(jnp.int32, (16, width), 0)
    b = lax.broadcasted_iota(jnp.int32, (16, width), 1)
    same = (b // channels == a) if all_lanes else (b == a * channels)
    return jnp.where(same & (a < H), 1.0, 0.0).astype(BF16)


def opened(part, width):
    half = part.shape[0] - 16
    rows = head_rows(width, True)

    def spread(n):
        return lax.dot_general(
            part[half:, n * half : (n + 1) * half],
            rows,
            (((0,), (0,)), ((), ())),
            preferred_element_type=F32,
        )

    return (part[:half].astype(F32), spread(0), spread(1) + spread(2))


def joined(parts, width):
    items = [opened(p, width) for p in parts]
    peak = items[0][1]
    for item in items[1:]:
        peak = jnp.maximum(peak, item[1])
    out, total = (0.0, 0.0)
    for o, m, t in items:
        factor = jnp.exp2(m - peak)
        out = out + o * factor
        total = total + t * factor
    return (out, peak, total)


def join_kernel(a, b, result):
    width = result.shape[1]
    half = result.shape[0] - 16
    out, peak, total = joined([a[...], b[...]], width)
    result[:half] = out.astype(BF16)
    high = total.astype(BF16)
    low = (total - high.astype(F32)).astype(BF16)
    rows = head_rows(width, False)
    for n, spread in enumerate((peak.astype(BF16), high, low)):
        flat = lax.dot_general(rows, spread, CONTRACT_LAST, preferred_element_type=F32)
        result[half:, n * half : (n + 1) * half] = flat.astype(BF16)
    result[half:, 3 * half :] = jnp.zeros((16, width - 3 * half), BF16)


def last_kernel(a, b, exits, result):
    width = result.shape[1]
    out, _, total = joined([a[...], b[...]], width)
    result[...] = dot((out / total).astype(BF16), exits[...]).astype(BF16)


def windows(tokens, side):
    cols, width = tokens.shape
    own = tokens.reshape(cols // BLK, BLK, width)
    side = side.reshape(1, BLK, width)
    after = jnp.concatenate([own[1:], side], axis=0)
    before = jnp.concatenate([side, own[:-1]], axis=0)
    place = lax.broadcasted_iota(jnp.int32, own.shape, 1)
    rim = jnp.where(place < BLK // 2, after, before)
    return jnp.concatenate([own, rim], axis=1).astype(BF16)


def copy_kernel(a, b):
    b[...] = a[...]


def own_kernel(x, side, gain, weights, keys, values, queries, key_win, value_win):
    rows, cols, width = x.shape
    channels = width // H
    ones = head_ones(256, channels)
    beside = token_norm(side[...].reshape(rows * BLK, width).astype(F32), gain[...])
    both = dot(beside, weights[:, width:])
    side_keys = head_norm(both[:, :width], ones, channels)
    side_values = both[:, width:]
    for i in range(rows // 2):
        tokens = x[2 * i : 2 * i + 2].reshape(2 * cols, width).astype(F32)
        normed = token_norm(tokens, gain[...])
        query = head_norm(dot(normed, weights[:, :width]), ones, channels)
        query = query.reshape(2, cols // BLK, BLK, width).transpose(1, 0, 2, 3)
        queries[:, 16 * i : 16 * i + 16, :] = query.reshape(cols // BLK, 16, width).astype(BF16)
    for r in range(rows):
        here = slice(r * cols, (r + 1) * cols)
        at = slice(r * BLK, (r + 1) * BLK)
        key_win[r] = windows(keys[here, :].astype(F32), side_keys[at])
        value_win[r] = windows(values[here, :].astype(F32), side_values[at])


def rim_kernel(up, down, gain, weights, key_rim, value_rim):
    lines, cols, width = up.shape
    channels = width // H
    ones = head_ones(256, channels)
    for n, ref in enumerate((up, down)):
        normed = token_norm(ref[...].astype(F32).reshape(lines * cols, width), gain[...])
        both = dot(normed, weights[:, width:])
        key = head_norm(both[:, :width], ones, channels)
        value = both[:, width:]
        for r in range(lines):
            at = slice(r * cols, (r + 1) * cols)
            key_rim[n * lines + r] = windows(key[at], key[at.start : at.start + BLK])
            value_rim[n * lines + r] = windows(value[at], value[at.start : at.start + BLK])


def halo_kernel(
    scale, place, x, corner, gain, weights, exits, queries, key_win, value_win, key_rim, value_rim,
    *refs, parts, stage
):
    rows, cols, width = x.shape
    channels = width // H
    ones = head_ones(256, channels)
    blocks = cols // BLK
    lines = rows + 2 * RIM
    order = parts[stage]
    if stage == 0:
        (attended,), key_end, value_end = (refs, None, None)
    else:
        first, attended, first_out, key_end, value_end = refs
        start = BLK * parts[0][0]
        count = BLK * len(parts[0])
        for i in range(rows // 4):
            here = slice(4 * i, 4 * i + 4)
            branch = dot(first[here].reshape(4 * count, width), exits[...])
            total = x[here, start : start + count].astype(F32) + branch.reshape(4, count, width)
            first_out[here] = total.astype(BF16)

        normed = token_norm(corner[...].reshape(2 * RIM * BLK, width).astype(F32), gain[...])
        both = dot(normed, weights[:, width:])
        corner_keys = head_norm(both[:, :width], ones, channels).reshape(2 * RIM, BLK, width)
        corner_values = both[:, width:].reshape(2 * RIM, BLK, width)
        sub = lax.broadcasted_iota(jnp.int32, (1, 16, 1), 1)
        for n, (block, beyond) in enumerate(
            ((0, sub >= 2 * BLK - RIM), (blocks - 1, sub < BLK + RIM))
        ):
            beyond = beyond & (sub >= BLK)
            for rim, tile, end in (
                (key_rim, corner_keys, key_end),
                (value_rim, corner_values, value_end),
            ):
                double = jnp.concatenate([tile, tile], axis=1)
                kept = rim[:, block].astype(F32)
                end[n] = jnp.where(beyond, double, kept).astype(BF16)

    spot = lax.broadcasted_iota(jnp.int32, (1, lines * 16), 1)
    line, sub = (spot // 16, spot % 16)
    upper = (line >= rows) & (line < rows + RIM)
    lower = line >= rows + RIM
    fixed = (sub == BLK + RIM) | (sub == BLK + RIM + 1)
    fixed = fixed | (upper & (place[0] == 0)) | (lower & (place[1] == 0))
    right = (sub >= BLK) & (sub < BLK + RIM)
    left = sub >= 2 * BLK - RIM
    group = 256
    per = group // channels
    owner = lax.broadcasted_iota(jnp.int32, (1, group), 1) // channels

    def one_block(block):
        gone = fixed
        if block == 0:
            gone = gone | (left & (place[2] == 0))
        if block == blocks - 1:
            gone = gone | (right & (place[3] == 0))
        bias = jnp.where(gone, NEG, 0.0)
        outs = []
        for g in range(width // group):
            at = slice(g * group, (g + 1) * group)

            def around(win, rim, end):
                if block == 0 or block == blocks - 1:
                    far = end[min(block, 1), :, :, at]
                else:
                    far = rim[:, block, :, at]
                own = win[:, block, :, at].reshape(rows * 16, group)
                return jnp.concatenate([own, far.reshape(2 * RIM * 16, group)], axis=0)

            query = queries[block, :, at]
            stacked = jnp.concatenate(
                [query * jnp.where(owner == h, 1.0, 0.0).astype(BF16) for h in range(per)], axis=0
            )
            key = around(key_win, key_rim, key_end)
            value = around(value_win, value_rim, value_end)
            scores = lax.dot_general(stacked, key, CONTRACT_LAST, preferred_element_type=F32)
            expos, totals = ([], [])
            n = BLK * BLK
            for h in range(per):
                s = scores[h * n : (h + 1) * n] * (scale[g * per + h] * (math.log2(math.e) / math.sqrt(channels))) + bias
                expo = jnp.exp2(s - jnp.max(s, axis=-1, keepdims=True))
                totals.append(jnp.sum(expo, axis=-1, keepdims=True))
                expos.append(expo.astype(BF16))
            mixed = dot(jnp.concatenate(expos, axis=0), value)
            out = jnp.zeros((n, group), F32)
            for h in range(per):
                out = jnp.where(owner == h, mixed[h * n : (h + 1) * n] / totals[h], out)
            outs.append(out)
        return jnp.concatenate(outs, axis=1).reshape(BLK, BLK, width)

    for i in range(len(order) // 2):
        pair = jnp.concatenate([one_block(order[2 * i]), one_block(order[2 * i + 1])], axis=1)
        attended[:, 16 * i : 16 * i + 16, :] = pair.astype(BF16)


def leave_kernel(x, exits, first, second, tokens_out, total, sems):
    rows, cols, width = x.shape
    count = second.shape[1] // 2
    middle = slice(count, cols - count)
    copies = [pltpu.make_async_copy(first, tokens_out.at[:, middle], sems.at[0])]
    copies[0].start()
    for i in range(rows // 4):
        here = slice(4 * i, 4 * i + 4)
        branch = dot(second[here].reshape(8 * count, width), exits[...])
        branch = branch.reshape(4, 2 * count, width)
        for n, at in enumerate((slice(0, count), slice(cols - count, cols))):
            from_x = x[here, at].astype(F32)
            total[here, n * count : (n + 1) * count] = (
                from_x + branch[:, n * count : (n + 1) * count]
            ).astype(BF16)
            copy = pltpu.make_async_copy(
                total.at[here, n * count : (n + 1) * count],
                tokens_out.at[here, at],
                sems.at[len(copies)],
            )
            copy.start()
            copies.append(copy)
    for copy in copies:
        copy.wait()


def call(kernel, outs, ins, scratch=(), megabytes=16, smem=0, far_outs=(), flops=1000):
    shapes = [jax.ShapeDtypeStruct(*o) for o in outs]
    return pl.pallas_call(
        kernel,
        out_shape=shapes,
        in_specs=[SMEM] * smem + [VMEM] * (len(ins) - smem),
        out_specs=[HBM if n in far_outs else VMEM for n in range(len(outs))],
        scratch_shapes=list(scratch),
        compiler_params=pltpu.CompilerParams(vmem_limit_bytes=megabytes * 1024 * 1024),
        cost_estimate=pl.CostEstimate(flops=flops, bytes_accessed=1000, transcendentals=0),
    )(*ins)


def per_device(
    crop_feature_grid,
    pixel_layernorm_gain,
    triple_projection_matrix,
    halo_exit_matrix,
    memory_slots,
    memory_layernorm_gain,
    memory_asking_matrix,
    memory_exit_matrix,
    branch_logit_multiplier,
):
    x = crop_feature_grid
    rows, cols, width = x.shape
    latents = memory_slots.shape[0]
    tall, wide = (lax.axis_size("rows"), lax.axis_size("cols"))
    row, col = (lax.axis_index("rows"), lax.axis_index("cols"))
    odd = row % 2 == 1
    place = jnp.stack([row > 0, row < tall - 1, col > 0, col < wide - 1, col > 0, odd])
    place = place.astype(jnp.int32)
    scale = branch_logit_multiplier
    gain = pixel_layernorm_gain.reshape(1, width)
    slot_gain = memory_layernorm_gain.reshape(1, width)
    weights = triple_projection_matrix

    near = [(i, i ^ 1) for i in range(tall)]
    far = [(i, j) for i in range(tall) if 0 <= (j := i - 1 if i % 2 == 0 else i + 1) < tall]
    swap = [(0, 1), (1, 0)]

    def edge(array):
        return jnp.where(col == 0, array[:, cols - BLK :], array[:, :BLK])

    (side,) = call(copy_kernel, [((rows, BLK, width), BF16)], (edge(x),), megabytes=2, flops=10**10)
    place, after, side = lax.optimization_barrier((place, x, side))
    top, bottom = (after[:RIM], after[rows - RIM :])
    near_rim = lax.ppermute(jnp.where(odd, top, bottom), "rows", near)
    far_rim = lax.ppermute(jnp.where(odd, bottom, top), "rows", far)
    side = lax.ppermute(side, "cols", swap)

    half = latents // 2
    tokens = rows * cols
    blocks = cols // BLK
    part = ((half + 16, width), BF16)
    keys, values, mine, other = call(
        latent_kernel,
        [((tokens, width), BF16), ((tokens, width), BF16), part, part],
        (scale, place, x, gain, weights, memory_slots, slot_gain, memory_asking_matrix),
        megabytes=24,
        smem=2,
    )
    queries, key_win, value_win = call(
        own_kernel,
        [
            ((blocks, rows * BLK, width), BF16),
            ((rows, blocks, 16, width), BF16),
            ((rows, blocks, 16, width), BF16),
        ],
        (x, side, gain, weights, keys, values),
        megabytes=16,
    )
    steps = [2**i for i in range(1, tall.bit_length() - 1)] + [1]
    parts = [mine, lax.ppermute(other, "cols", swap)]
    for n, step in enumerate(steps[:-1]):
        pairs = [(i, i ^ step) for i in range(tall)]
        (whole,) = call(join_kernel, [part], parts, megabytes=4)
        if n == len(steps) - 2:
            whole, near_rim, far_rim, queries = lax.optimization_barrier(
                (whole, near_rim, far_rim, queries)
            )
            up = jnp.where(odd, near_rim, far_rim)
            down = jnp.where(odd, far_rim, near_rim)
            corner = lax.ppermute(jnp.concatenate([edge(up), edge(down)]), "cols", swap)
        parts = [whole, lax.ppermute(whole, "rows", pairs)]

    rim = ((2 * RIM, blocks, 16, width), BF16)
    key_rim, value_rim = call(rim_kernel, [rim, rim], (up, down, gain, weights), megabytes=16)
    rest = blocks // 4
    parts_of = (
        list(range(rest, blocks - rest)),
        list(range(rest)) + list(range(blocks - rest, blocks)),
    )

    def halo(stage, outs, earlier=()):
        return call(
            functools.partial(halo_kernel, parts=parts_of, stage=stage),
            [(shape, BF16) for shape in outs],
            (
                scale,
                place,
                x,
                corner if stage else gain,
                gain,
                weights,
                halo_exit_matrix,
                queries,
                key_win,
                value_win,
                key_rim,
                value_rim,
                *earlier,
            ),
            scratch=[pltpu.VMEM((2, 2 * RIM, 16, width), BF16)] * (2 * stage),
            megabytes=24,
            smem=2,
        )

    inner = (rows, cols - 2 * rest * BLK, width)
    outer = (rows, 2 * rest * BLK, width)
    (first,) = halo(0, [inner])
    parts[1], first, corner = lax.optimization_barrier((parts[1], first, corner))
    (whole,) = call(join_kernel, [part], parts, megabytes=4)
    pairs = [(i, i ^ steps[-1]) for i in range(tall)]
    got = lax.ppermute(whole, "rows", pairs)
    second, first = halo(1, [outer, inner], (first,))
    got, second = lax.optimization_barrier((got, second))
    (mixed,) = call(
        last_kernel, [((half, width), BF16)], (whole, got, memory_exit_matrix), megabytes=6
    )
    (tokens_out,) = call(
        leave_kernel,
        [(x.shape, BF16)],
        (x, halo_exit_matrix, first, second),
        scratch=[
            pltpu.VMEM(outer, BF16),
            pltpu.SemaphoreType.DMA((1 + rows // 2,)),
        ],
        megabytes=12,
        far_outs=(0,),
    )
    theirs = lax.ppermute(mixed, "cols", swap)
    theirs, tokens_out = lax.optimization_barrier((theirs, tokens_out))
    latent_mix = jnp.where(
        col == 0, jnp.concatenate([mixed, theirs]), jnp.concatenate([theirs, mixed])
    )
    return (tokens_out, latent_mix)


def solution(mesh):
    return jax.shard_map(
        per_device,
        mesh=mesh,
        in_specs=(P(("grp", "rows"), "cols", None), P(), P(), P(), P(), P(), P(), P(), P()),
        out_specs=(P(("grp", "rows"), "cols", None), P("grp", None)),
        check_vma=False,
    )
```

```python
import functools
import math

import jax
import jax.numpy as jnp
from jax import lax
from jax.experimental import pallas as pl
from jax.experimental.pallas import tpu as pltpu
from jax.sharding import PartitionSpec as P

H = 8
BLK = 8
RIM = 3
F32 = jnp.float32
BF16 = jnp.bfloat16
NEG = -1e30
HBM = pl.BlockSpec(memory_space=pltpu.HBM)
VMEM = pl.BlockSpec(memory_space=pltpu.VMEM)
SMEM = pl.BlockSpec(memory_space=pltpu.SMEM)
CONTRACT_LAST = (((1,), (1,)), ((), ()))


def dot(a, b):
    return jnp.dot(a, b, preferred_element_type=F32)


def token_norm(floats, gain):
    scaled = floats * lax.rsqrt(jnp.mean(floats * floats, axis=-1, keepdims=True) + 1e-05)
    return (scaled * gain).astype(BF16)


def head_ones(width, channels):
    a = lax.broadcasted_iota(jnp.int32, (width, width), 0) // channels
    b = lax.broadcasted_iota(jnp.int32, (width, width), 1) // channels
    return jnp.where(a == b, 1.0, 0.0).astype(BF16)


def head_norm(floats, ones, channels):
    squares = floats * floats
    high = squares.astype(BF16)
    low = (squares - high.astype(F32)).astype(BF16)
    width = ones.shape[0]
    sums = [
        dot(high[:, i : i + width], ones) + dot(low[:, i : i + width], ones)
        for i in range(0, floats.shape[1], width)
    ]
    mean = jnp.concatenate(sums, axis=1) * (1.0 / channels)
    return floats * lax.rsqrt(mean + 1e-06)


def latent_kernel(
    scale, place, x, gain, weights, slots, slot_gain, asking, keys, values, mine, other
):
    rows, cols, width = x.shape
    heads = H
    channels = width // heads
    latents = slots.shape[0]
    ones = head_ones(256, channels)
    slot_normed = token_norm(slots[...].astype(F32), slot_gain[...])
    asked = head_norm(dot(slot_normed, asking[...]), ones, channels).astype(BF16)
    for i in range(rows // 2):
        tokens = x[2 * i : 2 * i + 2].reshape(2 * cols, width).astype(F32)
        normed = token_norm(tokens, gain[...])
        both = dot(normed, weights[:, width:])
        here = slice(2 * i * cols, (2 * i + 2) * cols)
        keys[here, :] = head_norm(both[:, :width], ones, channels).astype(BF16)
        values[here, :] = both[:, width:].astype(BF16)
    half = latents // 2
    first = place[4] == 0
    lanes = lax.broadcasted_iota(jnp.int32, (1, 128), 1)
    peaks = jnp.zeros((latents, 128), F32)
    totals = jnp.zeros((latents, 128), F32)
    per = 128 // channels
    for pair in range(heads // per):
        at = slice(pair * 128, (pair + 1) * 128)
        owner = lanes // channels
        query = jnp.concatenate(
            [asked[:, at] * jnp.where(owner == n, 1.0, 0.0).astype(BF16) for n in range(per)],
            axis=0,
        )
        scores = lax.dot_general(query, keys[:, at], CONTRACT_LAST, preferred_element_type=F32)
        expos = []
        for inner in range(per):
            head = pair * per + inner
            score = scores[inner * latents : (inner + 1) * latents] * (scale[head] * (math.log2(math.e) / math.sqrt(channels)))
            peak = jnp.max(score, axis=-1, keepdims=True)
            peak = (jnp.ceil(peak * 0.5) * 2.0).astype(BF16).astype(F32)
            expo = jnp.exp2(score - peak)
            total = jnp.sum(expo, axis=-1, keepdims=True)
            expos.append(expo.astype(BF16))
            peaks = jnp.where(lanes == head, peak, peaks)
            totals = jnp.where(lanes == head, total, totals)
        mixed = dot(jnp.concatenate(expos, axis=0), values[:, at])
        out = mixed[:latents]
        for inner in range(1, per):
            out = jnp.where(owner == inner, mixed[inner * latents : (inner + 1) * latents], out)
        out = out.astype(BF16)
        mine[:half, at] = jnp.where(first, out[:half], out[half:])
        other[:half, at] = jnp.where(first, out[half:], out[:half])
    high = totals.astype(BF16)
    low = (totals - high.astype(F32)).astype(BF16)
    sub = lax.broadcasted_iota(jnp.int32, (16, 128), 0)
    pick = jnp.where(sub == lax.broadcasted_iota(jnp.int32, (16, 128), 1), 1.0, 0.0)
    pick = jnp.where(sub < heads, pick, 0.0).astype(BF16)
    for n, columns in enumerate((peaks.astype(BF16), high, low)):
        flat = lax.dot_general(pick, columns, CONTRACT_LAST, preferred_element_type=F32)
        flat = flat.astype(BF16)
        at = slice(n * half, (n + 1) * half)
        mine[half:, at] = jnp.where(first, flat[:, :half], flat[:, half:])
        other[half:, at] = jnp.where(first, flat[:, half:], flat[:, :half])
    rest = slice(3 * half, width)
    mine[half:, rest] = jnp.zeros((16, width - 3 * half), BF16)
    other[half:, rest] = jnp.zeros((16, width - 3 * half), BF16)


def head_rows(width, all_lanes):
    channels = width // H
    a = lax.broadcasted_iota(jnp.int32, (16, width), 0)
    b = lax.broadcasted_iota(jnp.int32, (16, width), 1)
    same = (b // channels == a) if all_lanes else (b == a * channels)
    return jnp.where(same & (a < H), 1.0, 0.0).astype(BF16)


def opened(part, width):
    half = part.shape[0] - 16
    rows = head_rows(width, True)

    def spread(n):
        return lax.dot_general(
            part[half:, n * half : (n + 1) * half],
            rows,
            (((0,), (0,)), ((), ())),
            preferred_element_type=F32,
        )

    return (part[:half].astype(F32), spread(0), spread(1) + spread(2))


def joined(parts, width):
    items = [opened(p, width) for p in parts]
    peak = items[0][1]
    for item in items[1:]:
        peak = jnp.maximum(peak, item[1])
    out, total = (0.0, 0.0)
    for o, m, t in items:
        factor = jnp.exp2(m - peak)
        out = out + o * factor
        total = total + t * factor
    return (out, peak, total)


def join_kernel(a, b, result):
    width = result.shape[1]
    half = result.shape[0] - 16
    out, peak, total = joined([a[...], b[...]], width)
    result[:half] = out.astype(BF16)
    high = total.astype(BF16)
    low = (total - high.astype(F32)).astype(BF16)
    rows = head_rows(width, False)
    for n, spread in enumerate((peak.astype(BF16), high, low)):
        flat = lax.dot_general(rows, spread, CONTRACT_LAST, preferred_element_type=F32)
        result[half:, n * half : (n + 1) * half] = flat.astype(BF16)
    result[half:, 3 * half :] = jnp.zeros((16, width - 3 * half), BF16)


def last_kernel(a, b, exits, result):
    width = result.shape[1]
    out, _, total = joined([a[...], b[...]], width)
    result[...] = dot((out / total).astype(BF16), exits[...]).astype(BF16)


def windows(tokens, side):
    cols, width = tokens.shape
    own = tokens.reshape(cols // BLK, BLK, width)
    side = side.reshape(1, BLK, width)
    after = jnp.concatenate([own[1:], side], axis=0)
    before = jnp.concatenate([side, own[:-1]], axis=0)
    place = lax.broadcasted_iota(jnp.int32, own.shape, 1)
    rim = jnp.where(place < BLK // 2, after, before)
    return jnp.concatenate([own, rim], axis=1).astype(BF16)


def copy_kernel(a, b):
    b[...] = a[...]


def own_kernel(x, side, gain, weights, keys, values, queries, key_win, value_win):
    rows, cols, width = x.shape
    channels = width // H
    ones = head_ones(256, channels)
    beside = token_norm(side[...].reshape(rows * BLK, width).astype(F32), gain[...])
    both = dot(beside, weights[:, width:])
    side_keys = head_norm(both[:, :width], ones, channels)
    side_values = both[:, width:]
    for i in range(rows // 2):
        tokens = x[2 * i : 2 * i + 2].reshape(2 * cols, width).astype(F32)
        normed = token_norm(tokens, gain[...])
        query = head_norm(dot(normed, weights[:, :width]), ones, channels)
        query = query.reshape(2, cols // BLK, BLK, width).transpose(1, 0, 2, 3)
        queries[:, 16 * i : 16 * i + 16, :] = query.reshape(cols // BLK, 16, width).astype(BF16)
    for r in range(rows):
        here = slice(r * cols, (r + 1) * cols)
        at = slice(r * BLK, (r + 1) * BLK)
        key_win[r] = windows(keys[here, :].astype(F32), side_keys[at])
        value_win[r] = windows(values[here, :].astype(F32), side_values[at])


def rim_kernel(up, down, gain, weights, key_rim, value_rim):
    lines, cols, width = up.shape
    channels = width // H
    ones = head_ones(256, channels)
    for n, ref in enumerate((up, down)):
        normed = token_norm(ref[...].astype(F32).reshape(lines * cols, width), gain[...])
        both = dot(normed, weights[:, width:])
        key = head_norm(both[:, :width], ones, channels)
        value = both[:, width:]
        for r in range(lines):
            at = slice(r * cols, (r + 1) * cols)
            key_rim[n * lines + r] = windows(key[at], key[at.start : at.start + BLK])
            value_rim[n * lines + r] = windows(value[at], value[at.start : at.start + BLK])


def halo_kernel(
    scale, place, x, corner, gain, weights, exits, queries, key_win, value_win, key_rim, value_rim,
    *refs, parts, stage
):
    rows, cols, width = x.shape
    channels = width // H
    ones = head_ones(256, channels)
    blocks = cols // BLK
    lines = rows + 2 * RIM
    order = parts[stage]
    if stage == 0:
        (attended,), key_end, value_end = (refs, None, None)
    else:
        first, attended, first_out, key_end, value_end = refs
        start = BLK * parts[0][0]
        count = BLK * len(parts[0])
        for i in range(rows // 4):
            here = slice(4 * i, 4 * i + 4)
            branch = dot(first[here].reshape(4 * count, width), exits[...])
            total = x[here, start : start + count].astype(F32) + branch.reshape(4, count, width)
            first_out[here] = total.astype(BF16)

        normed = token_norm(corner[...].reshape(2 * RIM * BLK, width).astype(F32), gain[...])
        both = dot(normed, weights[:, width:])
        corner_keys = head_norm(both[:, :width], ones, channels).reshape(2 * RIM, BLK, width)
        corner_values = both[:, width:].reshape(2 * RIM, BLK, width)
        sub = lax.broadcasted_iota(jnp.int32, (1, 16, 1), 1)
        for n, (block, beyond) in enumerate(
            ((0, sub >= 2 * BLK - RIM), (blocks - 1, sub < BLK + RIM))
        ):
            beyond = beyond & (sub >= BLK)
            for rim, tile, end in (
                (key_rim, corner_keys, key_end),
                (value_rim, corner_values, value_end),
            ):
                double = jnp.concatenate([tile, tile], axis=1)
                kept = rim[:, block].astype(F32)
                end[n] = jnp.where(beyond, double, kept).astype(BF16)

    spot = lax.broadcasted_iota(jnp.int32, (1, lines * 16), 1)
    line, sub = (spot // 16, spot % 16)
    upper = (line >= rows) & (line < rows + RIM)
    lower = line >= rows + RIM
    fixed = (sub == BLK + RIM) | (sub == BLK + RIM + 1)
    fixed = fixed | (upper & (place[0] == 0)) | (lower & (place[1] == 0))
    right = (sub >= BLK) & (sub < BLK + RIM)
    left = sub >= 2 * BLK - RIM
    group = 256
    per = group // channels
    owner = lax.broadcasted_iota(jnp.int32, (1, group), 1) // channels

    def one_block(block):
        gone = fixed
        if block == 0:
            gone = gone | (left & (place[2] == 0))
        if block == blocks - 1:
            gone = gone | (right & (place[3] == 0))
        bias = jnp.where(gone, NEG, 0.0)
        outs = []
        for g in range(width // group):
            at = slice(g * group, (g + 1) * group)

            def around(win, rim, end):
                if block == 0 or block == blocks - 1:
                    far = end[min(block, 1), :, :, at]
                else:
                    far = rim[:, block, :, at]
                own = win[:, block, :, at].reshape(rows * 16, group)
                return jnp.concatenate([own, far.reshape(2 * RIM * 16, group)], axis=0)

            query = queries[block, :, at]
            stacked = jnp.concatenate(
                [query * jnp.where(owner == h, 1.0, 0.0).astype(BF16) for h in range(per)], axis=0
            )
            key = around(key_win, key_rim, key_end)
            value = around(value_win, value_rim, value_end)
            scores = lax.dot_general(stacked, key, CONTRACT_LAST, preferred_element_type=F32)
            expos, totals = ([], [])
            n = BLK * BLK
            for h in range(per):
                s = scores[h * n : (h + 1) * n] * (scale[g * per + h] * (math.log2(math.e) / math.sqrt(channels))) + bias
                expo = jnp.exp2(s - jnp.max(s, axis=-1, keepdims=True))
                totals.append(jnp.sum(expo, axis=-1, keepdims=True))
                expos.append(expo.astype(BF16))
            mixed = dot(jnp.concatenate(expos, axis=0), value)
            out = jnp.zeros((n, group), F32)
            for h in range(per):
                out = jnp.where(owner == h, mixed[h * n : (h + 1) * n] * (1.0 / totals[h]), out)
            outs.append(out)
        return jnp.concatenate(outs, axis=1).reshape(BLK, BLK, width)

    for i in range(len(order) // 2):
        pair = jnp.concatenate([one_block(order[2 * i]), one_block(order[2 * i + 1])], axis=1)
        attended[:, 16 * i : 16 * i + 16, :] = pair.astype(BF16)


def leave_kernel(x, exits, first, second, tokens_out, total, sems):
    rows, cols, width = x.shape
    count = second.shape[1] // 2
    middle = slice(count, cols - count)
    copies = [pltpu.make_async_copy(first, tokens_out.at[:, middle], sems.at[0])]
    copies[0].start()
    for i in range(rows // 4):
        here = slice(4 * i, 4 * i + 4)
        branch = dot(second[here].reshape(8 * count, width), exits[...])
        branch = branch.reshape(4, 2 * count, width)
        for n, at in enumerate((slice(0, count), slice(cols - count, cols))):
            from_x = x[here, at].astype(F32)
            total[here, n * count : (n + 1) * count] = (
                from_x + branch[:, n * count : (n + 1) * count]
            ).astype(BF16)
            copy = pltpu.make_async_copy(
                total.at[here, n * count : (n + 1) * count],
                tokens_out.at[here, at],
                sems.at[len(copies)],
            )
            copy.start()
            copies.append(copy)
    for copy in copies:
        copy.wait()


def call(kernel, outs, ins, scratch=(), megabytes=16, smem=0, far_outs=(), flops=1000):
    shapes = [jax.ShapeDtypeStruct(*o) for o in outs]
    return pl.pallas_call(
        kernel,
        out_shape=shapes,
        in_specs=[SMEM] * smem + [VMEM] * (len(ins) - smem),
        out_specs=[HBM if n in far_outs else VMEM for n in range(len(outs))],
        scratch_shapes=list(scratch),
        compiler_params=pltpu.CompilerParams(vmem_limit_bytes=megabytes * 1024 * 1024),
        cost_estimate=pl.CostEstimate(flops=flops, bytes_accessed=1000, transcendentals=0),
    )(*ins)


def per_device(
    crop_feature_grid,
    pixel_layernorm_gain,
    triple_projection_matrix,
    halo_exit_matrix,
    memory_slots,
    memory_layernorm_gain,
    memory_asking_matrix,
    memory_exit_matrix,
    branch_logit_multiplier,
):
    x = crop_feature_grid
    rows, cols, width = x.shape
    latents = memory_slots.shape[0]
    tall, wide = (lax.axis_size("rows"), lax.axis_size("cols"))
    row, col = (lax.axis_index("rows"), lax.axis_index("cols"))
    odd = row % 2 == 1
    place = jnp.stack([row > 0, row < tall - 1, col > 0, col < wide - 1, col > 0, odd])
    place = place.astype(jnp.int32)
    scale = branch_logit_multiplier
    gain = pixel_layernorm_gain.reshape(1, width)
    slot_gain = memory_layernorm_gain.reshape(1, width)
    weights = triple_projection_matrix

    near = [(i, i ^ 1) for i in range(tall)]
    far = [(i, j) for i in range(tall) if 0 <= (j := i - 1 if i % 2 == 0 else i + 1) < tall]
    swap = [(0, 1), (1, 0)]

    def edge(array):
        return jnp.where(col == 0, array[:, cols - BLK :], array[:, :BLK])

    (side,) = call(copy_kernel, [((rows, BLK, width), BF16)], (edge(x),), megabytes=2, flops=10**10)
    place, after, side = lax.optimization_barrier((place, x, side))
    top, bottom = (after[:RIM], after[rows - RIM :])
    near_rim = lax.ppermute(jnp.where(odd, top, bottom), "rows", near)
    far_rim = lax.ppermute(jnp.where(odd, bottom, top), "rows", far)
    side = lax.ppermute(side, "cols", swap)

    half = latents // 2
    tokens = rows * cols
    blocks = cols // BLK
    part = ((half + 16, width), BF16)
    keys, values, mine, other = call(
        latent_kernel,
        [((tokens, width), BF16), ((tokens, width), BF16), part, part],
        (scale, place, x, gain, weights, memory_slots, slot_gain, memory_asking_matrix),
        megabytes=24,
        smem=2,
    )
    queries, key_win, value_win = call(
        own_kernel,
        [
            ((blocks, rows * BLK, width), BF16),
            ((rows, blocks, 16, width), BF16),
            ((rows, blocks, 16, width), BF16),
        ],
        (x, side, gain, weights, keys, values),
        megabytes=16,
    )
    steps = [2**i for i in range(1, tall.bit_length() - 1)] + [1]
    parts = [mine, lax.ppermute(other, "cols", swap)]
    for n, step in enumerate(steps[:-1]):
        pairs = [(i, i ^ step) for i in range(tall)]
        (whole,) = call(join_kernel, [part], parts, megabytes=4)
        if n == len(steps) - 2:
            whole, near_rim, far_rim, queries = lax.optimization_barrier(
                (whole, near_rim, far_rim, queries)
            )
            up = jnp.where(odd, near_rim, far_rim)
            down = jnp.where(odd, far_rim, near_rim)
            corner = lax.ppermute(jnp.concatenate([edge(up), edge(down)]), "cols", swap)
        parts = [whole, lax.ppermute(whole, "rows", pairs)]

    rim = ((2 * RIM, blocks, 16, width), BF16)
    key_rim, value_rim = call(rim_kernel, [rim, rim], (up, down, gain, weights), megabytes=16)
    rest = blocks // 4
    parts_of = (
        list(range(rest, blocks - rest)),
        list(range(rest)) + list(range(blocks - rest, blocks)),
    )

    def halo(stage, outs, earlier=()):
        return call(
            functools.partial(halo_kernel, parts=parts_of, stage=stage),
            [(shape, BF16) for shape in outs],
            (
                scale,
                place,
                x,
                corner if stage else gain,
                gain,
                weights,
                halo_exit_matrix,
                queries,
                key_win,
                value_win,
                key_rim,
                value_rim,
                *earlier,
            ),
            scratch=[pltpu.VMEM((2, 2 * RIM, 16, width), BF16)] * (2 * stage),
            megabytes=24,
            smem=2,
        )

    inner = (rows, cols - 2 * rest * BLK, width)
    outer = (rows, 2 * rest * BLK, width)
    (first,) = halo(0, [inner])
    parts[1], first, corner = lax.optimization_barrier((parts[1], first, corner))
    (whole,) = call(join_kernel, [part], parts, megabytes=4)
    pairs = [(i, i ^ steps[-1]) for i in range(tall)]
    got = lax.ppermute(whole, "rows", pairs)
    second, first = halo(1, [outer, inner], (first,))
    got, second = lax.optimization_barrier((got, second))
    (mixed,) = call(
        last_kernel, [((half, width), BF16)], (whole, got, memory_exit_matrix), megabytes=6
    )
    (tokens_out,) = call(
        leave_kernel,
        [(x.shape, BF16)],
        (x, halo_exit_matrix, first, second),
        scratch=[
            pltpu.VMEM(outer, BF16),
            pltpu.SemaphoreType.DMA((1 + rows // 2,)),
        ],
        megabytes=12,
        far_outs=(0,),
    )
    theirs = lax.ppermute(mixed, "cols", swap)
    theirs, tokens_out = lax.optimization_barrier((theirs, tokens_out))
    latent_mix = jnp.where(
        col == 0, jnp.concatenate([mixed, theirs]), jnp.concatenate([theirs, mixed])
    )
    return (tokens_out, latent_mix)


def solution(mesh):
    return jax.shard_map(
        per_device,
        mesh=mesh,
        in_specs=(P(("grp", "rows"), "cols", None), P(), P(), P(), P(), P(), P(), P(), P()),
        out_specs=(P(("grp", "rows"), "cols", None), P("grp", None)),
        check_vma=False,
    )
```
